32 devices in a mesh: tile: 16 (over z, x, core), mlp: 2 (over y).
Axes of the slice: x: 2, y: 2, z: 4, core: 2. Of those that a mesh axis runs over, the one named last changes fastest.
Arguments:
- features: bfloat16 [16, 512, 2, 2, 256], P('tile', 'mlp'), may hold values from -6 to 6
- w_in: bfloat16 [256, 1024], P(None, 'mlp'), may hold values from -0.375 to 0.375
- w_out: bfloat16 [1024, 256], P('mlp'), may hold values from -0.1875 to 0.1875
- bilinear: bfloat16 [256, 256], replicated, may hold values from -0.375 to 0.375
- partner: int32 [16, 2, 512], replicated, may hold values from 0 to 13823
- counts: int32 [16, 2, 2], replicated, may hold values from 128 to 512
Outputs:
- pair_loss: float32 [], replicated
- grad_in: float32 [256, 1024], P(None, 'mlp')
- grad_out: float32 [1024, 256], P('mlp')
- grad_bilinear: float32 [256, 256], replicated
The draws below stay inside these ranges and needn't reach their ends.
All inputs are finite; a program needn't handle non-finite values.
Results may differ from the reference program's by a relative error of at most 0.0024.
The reference program's roundings to bfloat16 on the way (of `active`, `embedded`, `query`, `slope`, `query_grad`, `embed_grad` and `hidden_grad`) count: a program that leaves them out, or rounds other values in their place, can miss the bound.
Values may be sent and summed in bfloat16 or wider, within the bound.
No kernel may reach another device: no remote copies, remote signals or barrier semaphores. Data moves between devices by JAX's collectives and lax.ppermute only.
A program may use at most 64 MiB of HBM per device.

```python
import jax
import jax.numpy as jnp

F = 256
HID = 1024
S = 512
BLOCKS = 16
HEAVY = 3456
PRE_SITES = 16384


def draw_counts(key, part):
    values = jax.random.randint(key, (BLOCKS, 2, 2), S // 4, S + 1, dtype=jnp.int32)
    values = values.at[0, 0, 0].set(S)
    return values.at[0, 1, 1].set(S // 4)


def with_ends(drawn, key, least, high):
    spot = [jax.random.randint(jax.random.fold_in(key, axis), (), 0, length) for axis, length in enumerate(drawn.shape)]
    widest = drawn.shape.index(max(drawn.shape))
    next_to = spot[:widest] + [(spot[widest] + 1) % drawn.shape[widest]] + spot[widest + 1:]
    return drawn.at[tuple(spot)].set(least).at[tuple(next_to)].set(high)


def block_levels(own_key, dims, pieces, smallest, top_value):
    factor_of, own = 1.0, jax.random.fold_in(own_key, 6)
    for position, blocks in pieces:
        draws = jnp.exp(jax.random.uniform(jax.random.fold_in(own, position), (blocks,), jnp.float32, smallest / len(pieces), top_value / len(pieces)))
        factor_of = factor_of * jnp.repeat(draws, dims[position] // blocks).reshape([-1 if axis == position else 1 for axis in range(len(dims))])
    return factor_of


def centred(stream_key, dims, scale, limit, pieces=(), kind=jnp.bfloat16):
    factor_of = block_levels(stream_key, dims, pieces, -0.22, 0.18) if pieces else 1.0
    drawn = jax.random.normal(stream_key, dims, jnp.float32) * scale * factor_of
    return jnp.minimum(jnp.maximum(drawn, -limit), limit).astype(kind)


def setup_inputs(seed: int = 0) -> dict:
    splits = jax.random.split(jax.random.key(seed), 7)
    features = centred(splits[0], (BLOCKS, S, 2, 2, F), 1.0, 6.0, ((0, 16), (1, 2)))
    w_in = centred(splits[1], (F, HID), F ** -0.5, 0.375, ((1, 2),))
    w_out = centred(splits[2], (HID, F), HID ** -0.5, 0.1875, ((0, 2),))
    bilinear = centred(splits[3], (F, F), F ** -0.5, 0.375)
    partner = with_ends(jax.random.randint(splits[4], (BLOCKS, 2, S), 0, 27 * S), jax.random.fold_in(splits[4], 1), 0, (27 * S) - 1).astype(jnp.int32)
    counts = draw_counts(jax.random.fold_in(splits[6], 71), 0)
    return {"features": features, "w_in": w_in, "w_out": w_out, "bilinear": bilinear, "partner": partner, "counts": counts}


def to_grid(array):
    depth_count = array.shape[0] // 8
    rest_shape = array.shape[2:]
    shaped = array.reshape((2, 4, depth_count, 2) + rest_shape)
    moved = jnp.moveaxis(shaped, 3, 1)
    return moved.reshape((4, 4, depth_count) + rest_shape)

def from_grid(grid):
    depth_count = grid.shape[2]
    rest_shape = grid.shape[3:]
    shaped = grid.reshape((2, 2, 4, depth_count) + rest_shape)
    moved = jnp.moveaxis(shaped, 1, 3)
    return moved.reshape((8 * depth_count, 2) + rest_shape)

def shifted(grid, step_x, step_y, step_z):
    padding = [(1, 1)] * 3 + [(0, 0)] * (grid.ndim - 3)
    padded = jnp.pad(grid, padding)
    return padded[1 + step_x:1 + step_x + grid.shape[0], 1 + step_y:1 + step_y + grid.shape[1], 1 + step_z:1 + step_z + grid.shape[2]]

def reference(features, w_in, w_out, bilinear, partner, counts):
    blocks_here = features.shape[0]
    inputs = features.reshape(blocks_here, S, 4, F).astype(jnp.float32)
    hidden = jnp.einsum('bscf,fh->bsch', inputs, w_in.astype(jnp.float32))
    active = jax.nn.gelu(hidden).astype(jnp.bfloat16)
    mixed_rows = jnp.einsum('bsch,hf->bscf', active.astype(jnp.float32), w_out.astype(jnp.float32))
    embedded = (inputs + mixed_rows).astype(jnp.bfloat16)
    pre_rows = embedded[:, :, 0::2]
    post_rows = embedded[:, :, 1::2]
    query = jnp.einsum('bsuf,fg->bsug', pre_rows.astype(jnp.float32), bilinear.astype(jnp.float32)).astype(jnp.bfloat16)
    query_grid = to_grid(jnp.moveaxis(query, 2, 1)).astype(jnp.float32)
    post_grid = to_grid(jnp.moveaxis(post_rows, 2, 1)).astype(jnp.float32)
    partner_grid = to_grid(partner)
    pre_count = to_grid(counts[:, :, 0])
    post_count = to_grid(counts[:, :, 1])
    site_index = jnp.arange(S, dtype=jnp.int32)
    pre_valid = site_index < pre_count[..., None]
    score_scale = F ** (-0.5)
    factor = score_scale / PRE_SITES
    loss_sum = jnp.zeros((), jnp.float32)
    query_grad = jnp.zeros(query_grid.shape, jnp.float32)
    post_grad = jnp.zeros(post_grid.shape, jnp.float32)
    for step_x in (-1, 0, 1):
        for step_y in (-1, 0, 1):
            for step_z in (-1, 0, 1):
                others = shifted(post_grid, step_x, step_y, step_z)
                other_valid = site_index < shifted(post_count, step_x, step_y, step_z)[..., None]
                code = (step_x + 1) * 9 + (step_y + 1) * 3 + step_z + 1
                score = jnp.einsum('xyzif,xyzjf->xyzij', query_grid, others) * score_scale
                target = (partner_grid[..., :, None] == code * S + site_index).astype(jnp.float32)
                weight = (pre_valid[..., :, None] & other_valid[..., None, :]).astype(jnp.float32)
                chance = jax.nn.sigmoid(score)
                missed = HEAVY * target * jnp.log1p(jnp.exp(-score))
                spurious = (1.0 - target) * jnp.log1p(jnp.exp(score))
                loss_sum = loss_sum + jnp.sum(weight * (missed + spurious))
                signed = (1.0 - target) * chance - HEAVY * target * (1.0 - chance)
                slope = (weight * signed * factor).astype(jnp.bfloat16).astype(jnp.float32)
                query_grad = query_grad + jnp.einsum('xyzij,xyzjf->xyzif', slope, others)
                back = jnp.einsum('xyzij,xyzif->xyzjf', slope, query_grid)
                post_grad = post_grad + shifted(back, -step_x, -step_y, -step_z)
    query_back = jnp.moveaxis(from_grid(query_grad), 1, 2).astype(jnp.bfloat16).astype(jnp.float32)
    post_back = jnp.moveaxis(from_grid(post_grad), 1, 2)
    grad_bilinear = jnp.einsum('bsuf,bsug->fg', pre_rows.astype(jnp.float32), query_back)
    pre_back = jnp.einsum('bsug,fg->bsuf', query_back, bilinear.astype(jnp.float32))
    embed_grad = jnp.stack([pre_back[:, :, 0], post_back[:, :, 0], pre_back[:, :, 1], post_back[:, :, 1]], axis=2).astype(jnp.bfloat16).astype(jnp.float32)
    active_grad = jnp.einsum('bscf,hf->bsch', embed_grad, w_out.astype(jnp.float32))
    unused, pullback = jax.vjp(jax.nn.gelu, hidden)
    hidden_grad = pullback(active_grad)[0].astype(jnp.bfloat16).astype(jnp.float32)
    grad_in = jnp.einsum('bscf,bsch->fh', inputs, hidden_grad)
    grad_out = jnp.einsum('bsch,bscf->hf', active.astype(jnp.float32), embed_grad)
    pair_loss = loss_sum / (PRE_SITES * 27 * S)
    return (pair_loss, grad_in, grad_out, grad_bilinear)
```

```python
import functools

import jax
import jax.numpy as jnp
from jax import lax
from jax.experimental import pallas as pl
from jax.experimental.pallas import tpu as pltpu
from jax.sharding import PartitionSpec as P

f32 = jnp.float32
bf16 = jnp.bfloat16
OFF = -1e30
VMEM = pl.BlockSpec(memory_space=pltpu.VMEM)
SMEM = pl.BlockSpec(memory_space=pltpu.SMEM)


def dot(a, b):
    return lax.dot_general(a, b, (((1,), (0,)), ((), ())), preferred_element_type=f32)


def moved(array, axis, target):
    peers = lax.axis_size(axis)
    pairs = [(i, target(i)) for i in range(peers) if target(i) is not None]
    return lax.ppermute(array, axis, pairs)


def over_mlp(array):
    groups = lax.axis_size("mlp")
    if groups == 2:
        return [array, moved(array, "mlp", lambda i: 1 - i)]
    gathered = lax.all_gather(array, "mlp", axis=0)
    member = lax.axis_index("mlp")
    order = [lax.rem(member + step, groups) for step in range(groups)]
    return [lax.dynamic_index_in_dim(gathered, g, 0, keepdims=False) for g in order]


def owner(meta, step, groups):
    return lax.rem(meta[1] + step, groups)


def call(kernel, name, outs, operands, flops=0, scratch=(), aliases=None):
    specs = [SMEM if o.dtype == jnp.int32 and o.ndim == 1 else VMEM for o in operands]
    size = sum(o.size * o.dtype.itemsize for o in operands)
    return pl.pallas_call(
        kernel,
        out_shape=[jax.ShapeDtypeStruct(shape, kind) for shape, kind in outs],
        in_specs=specs,
        out_specs=[VMEM] * len(outs),
        scratch_shapes=list(scratch),
        input_output_aliases=aliases or {},
        compiler_params=pltpu.CompilerParams(vmem_limit_bytes=40 * 1024 * 1024),
        cost_estimate=pl.CostEstimate(flops=flops, bytes_accessed=size, transcendentals=0),
        name=name,
    )(*operands)


def summed(arrays, places, kind, name):
    def kernel(*refs):
        for (first, count), out in zip(places, refs[len(arrays) :], strict=True):
            for t in range(count):
                total = None
                for ref in refs[: len(arrays)]:
                    if first + t < ref.shape[0]:
                        part = ref[first + t].astype(f32)
                        total = part if total is None else total + part
                out[t] = total.astype(kind)

    shape = arrays[0].shape[1:]
    return call(kernel, name, [((count, *shape), kind) for unused, count in places], arrays)


def sub_tile(xb, t):
    return 1 - xb if t == 0 else xb


def gelu_parts(h):
    c = 0.7978845608028654
    square = h * h
    bend = jnp.tanh(c * (h + 0.044715 * (square * h)))
    whole = 0.5 * (1.0 + bend)
    slope = whole + 0.5 * h * (1.0 - bend * bend) * (c * (1.0 + 3 * 0.044715 * square))
    return h * whole, slope


def mlp_kernel(kinds, ready, near, groups, *refs):
    refs = list(refs)
    meta, x_ref = refs[:2]
    del refs[:2]
    near_ref = refs.pop() if near else None
    out_ref = refs.pop()
    start_ref = refs.pop(0) if ready else None
    xb = meta[2]
    for place, kind in enumerate(kinds):
        for t in range(2):
            x = x_ref[kind, sub_tile(xb, t)]
            total = start_ref[kind, t] if ready else x.astype(f32)
            for g in range(groups):
                hidden = dot(x, refs[2 * g][...])
                active = gelu_parts(hidden)[0].astype(bf16)
                total = total + dot(active, refs[2 * g + 1][...])
            if len(kinds) == 1:
                out_ref[t] = total.astype(out_ref.dtype)
                if near and t == 0:
                    near_ref[0] = total.astype(out_ref.dtype)
            else:
                out_ref[place, t] = total.astype(out_ref.dtype)


def hidden_kernel(groups, meta, w_in_ref, *refs):
    w_t = w_in_ref[...].T
    outs = refs[groups:]
    for kind in range(2):
        for g in range(groups):
            for u in range(2):
                active, slope = gelu_parts(dot(w_t, refs[g][kind, u].T))
                outs[2 * kind][g, u] = active.astype(bf16)
                outs[2 * kind + 1][g, u] = slope


def weight_part(back, x, active_t, slope_t, w_out, sums):
    active_grad = dot(w_out, back.T)
    hidden_grad = (active_grad * slope_t).astype(bf16)
    return sums[0] + dot(hidden_grad, x), sums[1] + dot(active_t, back)


def pre_kernel(groups, meta, w_out_ref, bil_ref, active_ref, slope_ref, *refs):
    query_refs, pre_refs, x_refs = refs[:groups], refs[groups : 2 * groups], refs[2 * groups : 3 * groups]
    in_ref, out_ref, bil_grad_ref, loss_ref, pre_all, back_all = refs[3 * groups :]
    rows = pre_refs[0].shape[1]
    site_rows = rows * groups
    xb = meta[2]
    bil_t = bil_ref[...].T
    bil_grad = jnp.zeros(bil_grad_ref.shape, f32)
    sums = (jnp.zeros(in_ref.shape, f32), jnp.zeros(out_ref.shape, f32))
    for a in range(2):
        total = query_refs[0][a * site_rows : (a + 1) * site_rows]
        for ref in query_refs[1:]:
            total = total + ref[a * site_rows : (a + 1) * site_rows]
        query_back = total.astype(bf16)
        for g in range(groups):
            place = pl.ds(pl.multiple_of(owner(meta, g, groups) * rows, rows), rows)
            pre_all[a, place, :] = pre_refs[g][a]
        for g in range(groups):
            place = slice(g * rows, (g + 1) * rows)
            bil_grad = bil_grad + dot(pre_all[a, place, :].T, query_back[place])
        back_all[a] = dot(query_back, bil_t).astype(bf16)
        u = sub_tile(xb, a)
        for g in range(groups):
            place = pl.ds(pl.multiple_of(owner(meta, g, groups) * rows, rows), rows)
            back = back_all[a, place, :]
            sums = weight_part(back, x_refs[g][0, u], active_ref[g, u], slope_ref[g, u], w_out_ref[...], sums)
    in_ref[...], out_ref[...] = sums
    bil_grad_ref[...] = bil_grad
    loss = query_refs[0][2 * site_rows :]
    for ref in query_refs[1:]:
        loss = loss + ref[2 * site_rows :]
    loss_ref[...] = loss


def post_kernel(groups, meta, w_out_ref, active_ref, slope_ref, in0, out0, bil0, loss0, *refs):
    near_refs, far_refs, x_refs = refs[:groups], refs[groups : 2 * groups], refs[2 * groups : 3 * groups]
    mine_ref, other_ref, whole = refs[3 * groups :]
    xb = meta[2]
    core = lax.rem(meta[0], 2)
    sums = (in0[...], out0[...])
    for t in range(2):
        u = sub_tile(xb, t)
        for g in range(groups):
            back = (near_refs, far_refs)[t][g][0]
            sums = weight_part(back, x_refs[g][1, u], active_ref[g, u], slope_ref[g, u], w_out_ref[...], sums)
    hid = in0.shape[0]
    half = mine_ref.shape[0]
    whole[:hid] = sums[0]
    whole[hid : 2 * hid] = sums[1]
    whole[2 * hid :] = bil0[...]
    mine_ref[...] = whole[pl.ds(pl.multiple_of(core * half, 16), half), :]
    other_ref[:half] = whole[pl.ds(pl.multiple_of((1 - core) * half, 16), half), :]
    other_ref[half:] = loss0[...]


def halves_kernel(meta, mine_ref, other_ref, loss0, sent_ref, kept_ref, whole):
    rows = kept_ref.shape[0] - 8
    half = mine_ref.shape[0]
    whole[...] = mine_ref[...] + other_ref[:half]
    sent_ref[...] = whole[...].astype(sent_ref.dtype)
    kept_ref[rows:] = loss0[...] + other_ref[half:]
    kept_ref[:rows] = whole[pl.ds(pl.multiple_of(meta[0] // 2 * rows, 16), rows), :]


def total_kernel(meta, got_ref, kept_ref, out_ref):
    rows = kept_ref.shape[0] - 8
    chips = got_ref.shape[0] // rows
    total = kept_ref[:rows]
    for n in range(chips):
        piece = got_ref[n * rows : (n + 1) * rows, :].astype(f32)
        total = total + jnp.where(n == meta[0] // 2, 0.0, piece)
    for n in range(chips):
        first = n * (rows + 8)
        out_ref[first : first + rows, :] = total
        out_ref[first + rows : first + rows + 8, :] = kept_ref[rows:]


def last_kernel(chips, share, meta, mine_ref, other_ref, in_ref, out_ref, bil_ref, loss_ref, whole):
    core = lax.rem(meta[0], 2)
    half = whole.shape[0] // 2
    rows = half // chips
    loss = jnp.zeros((8, 128), f32)
    for n in range(chips):
        first = n * (rows + 8)
        for ref, side in ((mine_ref, core), (other_ref, 1 - core)):
            place = side * half + n * rows
            whole[pl.ds(pl.multiple_of(place, 8), rows), :] = ref[first : first + rows, :]
        loss = loss + mine_ref[first + rows : first + rows + 8, :128]
    hid = out_ref.shape[0]
    in_ref[...] = whole[:hid].T
    out_ref[...] = whole[hid : 2 * hid]
    bil_ref[...] = whole[2 * hid :]
    loss_ref[...] = loss * share


def pair_kernel(slots, foreign, first, last, groups, site_rows, depth, heavy, out_scale, *refs):
    refs = list(refs)

    def take(count):
        taken = refs[:count]
        del refs[:count]
        return taken

    meta, counts, label_ref = take(3)
    if first:
        bil_ref = take(1)[0]
        pre_refs = take(groups)
    else:
        q_ref, qt_ref, acc_in, loss_in, hit_in, found_in = take(6)
    post_refs = take(len(slots))
    z_list = list(dict.fromkeys(z for unused, z in slots))
    grad_refs = dict(zip(z_list, take(len(z_list)), strict=True))
    if first:
        q_ref, qt_ref = take(2)
    if last:
        out_ref, acc, loss_ref, hit_ref, found_ref = refs
    else:
        acc, loss_ref, hit_ref, found_ref = refs
    tile_here, member, xb = meta[0], meta[1], meta[2]
    yg = lax.rem(tile_here // depth, 4)
    zg = lax.rem(tile_here, depth)
    toward = 1 - 2 * xb
    rows = post_refs[0].shape[1]
    width = post_refs[0].shape[2]
    if first:
        scale = jnp.asarray(width ** (-0.5), bf16)
        for a in range(2):
            for g in range(groups):
                part = dot(pre_refs[g][a], bil_ref[...]).astype(bf16)
                place = pl.ds(pl.multiple_of(owner(meta, g, groups) * rows, rows), rows)
                q_ref[a, place, :] = part
            qt_ref[a] = (q_ref[a] * scale).T
        acc[...] = jnp.zeros_like(acc)
        loss_ref[...] = jnp.zeros_like(loss_ref)
        hit_ref[...] = jnp.zeros_like(hit_ref)
        found_ref[...] = jnp.zeros_like(found_ref)
    elif last:
        acc[...] = acc_in[...]
        loss_ref[...] = loss_in[...]
        hit_ref[...] = hit_in[...]
        found_ref[...] = found_in[...]
    j_own = lax.broadcasted_iota(jnp.int32, (rows, site_rows), 0)
    j_col = lax.broadcasted_iota(jnp.int32, (rows, 128), 0)
    i_row = lax.broadcasted_iota(jnp.int32, (1, site_rows), 1)
    step = rows // (8 if rows >= 128 else 4)
    i_ok = [i_row < counts[tile_here * 4 + sub_tile(xb, a) * 2] for a in (0, 1)]
    i_bias = [jnp.where(ok, 0.0, OFF).astype(f32) for ok in i_ok]
    if foreign:
        nz = sum(1 for dy, unused in slots if dy == 0)
        chunks = [[(n, 0) for n in range(k, k + nz)] for k in range(0, len(slots), nz)]
    else:
        chunks = [[(n, 0), (n, 1)] for n in range(len(slots))]
    for chunk in chunks:
        post = jnp.concatenate([post_refs[n][t] for n, t in chunk], 0)
        post_t = post.T
        places = []
        for n, t in chunk:
            dy, z_slot = slots[n]
            if depth == 2:
                z_other = zg if z_slot == 0 else 1 - zg
            else:
                z_other = zg + z_slot
            x_other = 1 - xb if foreign else xb
            y_other = yg + dy
            inside = (y_other >= 0) & (y_other < 4) & (z_other >= 0) & (z_other < depth)
            source = jnp.where(inside, x_other * 4 * depth + y_other * depth + z_other, tile_here)
            valid = jnp.clip(counts[source * 4 + sub_tile(x_other, t) * 2 + 1] - member * rows, 0, rows)
            places.append((t, dy, z_other - zg, jnp.where(inside, valid, 0)))
        j_bias = jnp.concatenate([jnp.where(j_col < place[3], 0.0, OFF).astype(f32) for place in places], 0)
        j_bias = jnp.concatenate([j_bias] * (site_rows // 128), 1)
        total = None
        for a in (0,) if foreign else (0, 1):
            targets = []
            for t, dy, dz, valid in places:
                dx = toward if foreign else 0 if t == a else -toward if a == 0 else toward
                base = ((dx + 1) * 9 + (dy + 1) * 3 + dz + 1) * site_rows + member * rows
                key = label_ref[sub_tile(xb, a)] - base
                key = jnp.where(i_ok[a] & (key < valid), key, -1)
                found_ref[a] += jnp.where(key >= 0, 1.0, 0.0)
                targets.append(j_own == key)
            target = jnp.concatenate(targets, 0)
            s = dot(post, qt_ref[a]) + j_bias + i_bias[a]
            e = jnp.exp(-jnp.abs(s))
            w = 1.0 + e
            r = pl.reciprocal(w, approx=True)
            chance = jnp.where(s >= 0.0, r, e * r)
            slope = jnp.where(target, (chance - 1.0) * heavy, chance).astype(bf16)
            part = dot(slope, q_ref[a])
            total = part if total is None else total + part
            acc[a] += dot(post_t, slope)
            piece = hit = None
            for k in range(len(chunk)):
                product = small = above = None
                for g in range(k * rows, (k + 1) * rows, step):
                    here = slice(g, g + step)
                    more = jnp.maximum(s[here], 0.0)
                    found = jnp.where(target[here], s[here], 0.0)
                    product = w[here] if product is None else product * w[here]
                    small = e[here] if small is None else small + e[here]
                    above = more if above is None else above + more
                    hit = found if hit is None else hit + found
                loss = above + jnp.where(small < 1e-3, small, jnp.log(product))
                piece = loss if piece is None else piece + loss
            loss_ref[...] += jnp.sum(piece.reshape(step // 8, 8, site_rows), 0)
            hit_ref[a] += jnp.sum(hit.reshape(step // 8, 8, site_rows), 0)
        for k, (n, t) in enumerate(chunk):
            dy, z_slot = slots[n]
            place = [other for other, z in slots if z == z_slot].index(dy) * post_refs[n].shape[0] + t
            grad_refs[z_slot][place] = total[k * rows : (k + 1) * rows] * out_scale
    if last:
        total = jnp.sum(loss_ref[...])
        for a in range(2):
            out_ref[a * site_rows : (a + 1) * site_rows] = (acc[a] * out_scale).T
            score = jnp.sum(hit_ref[a], 0, keepdims=True)
            soft = jnp.log1p(jnp.exp(-jnp.abs(score)))
            missed = heavy * (jnp.maximum(-score, 0.0) + soft) - (jnp.maximum(score, 0.0) + soft)
            total = total + jnp.sum(jnp.where(found_ref[a] > 0.0, missed, 0.0))
        out_ref[2 * site_rows :] = jnp.full((8, width), total, f32)


def pair_call(name, slots, foreign, first, last, operands, posts, sizes):
    tiles, rows, width = posts[0].shape
    groups, site_rows = sizes[0], sizes[1]
    kernel = functools.partial(pair_kernel, slots, foreign, first, last, *sizes)
    state = [
        ((2, width, site_rows), f32),
        ((8, site_rows), f32),
        ((2, 8, site_rows), f32),
        ((2, 1, site_rows), f32),
    ]
    z_count = len(set(z for unused, z in slots))
    outs = [((tiles * len(slots) // z_count, rows, width), f32)] * z_count
    if first:
        outs += [((2, site_rows, width), bf16), ((2, width, site_rows), bf16)]
    if last:
        outs += [((2 * site_rows + 8, width), f32)]
    else:
        outs += state
    pairs = len(slots) * (1 if foreign else 4)
    aliases = {} if first or last else {5 + n: z_count + n for n in range(4)}
    results = call(
        kernel,
        name,
        outs,
        operands + posts,
        flops=pairs * rows * site_rows * width * 40,
        scratch=[pltpu.VMEM(shape, kind) for shape, kind in state] if last else (),
        aliases=aliases,
    )
    return list(results[:z_count]), list(results[z_count:])


def after(array, *others):
    return lax.optimization_barrier((array, *others))[0]


def local(features, w_in, w_out, bilinear, partner, counts):
    row_part = features.shape[1]
    width = features.shape[4]
    hid = w_in.shape[1]
    groups = lax.axis_size("mlp")
    site_rows = row_part * groups
    tile_count = lax.axis_size("tile")
    depth = tile_count // 8
    tile_here = lax.axis_index("tile")
    member = lax.axis_index("mlp")
    xb = tile_here // (4 * depth)
    heavy = float(27 * site_rows // 4)
    out_scale = width ** (-0.5) / (2 * tile_count * site_rows)
    half = tile_count // 2

    def side(i):
        return i ^ half

    def along_y(step):
        return lambda i: i + step * depth if 0 <= i // depth % 4 + step < 4 else None

    def both(step):
        return lambda i: None if along_y(step)(i) is None else along_y(step)(i) ^ half

    z_slots = (0, 1) if depth == 2 else (0, -1, 1)

    def along_z(slot):
        if depth == 2:
            return lambda i: i ^ 1
        return lambda i: i - slot if 0 <= i % depth - slot < depth else None

    def back_z(slot):
        return along_z(slot if depth == 2 else -slot)

    def from_z(array):
        return [moved(array, "tile", along_z(slot)) for slot in z_slots[1:]]

    w_ins, w_outs = over_mlp(w_in), over_mlp(w_out)
    meta = jnp.stack([tile_here, member, xb]).astype(jnp.int32)
    x = jnp.transpose(features[0], (2, 1, 0, 3))
    labels = lax.dynamic_index_in_dim(partner, tile_here, 0, keepdims=False)[:, None, :]
    flat_counts = counts.reshape(-1)
    rows4 = (2, 2, row_part, width)
    rows3 = (2, row_part, width)
    flops = 4 * row_part * width * hid * 4
    begun = call(
        functools.partial(mlp_kernel, (0, 1), False, False, 1), "mlp_own", [(rows4, f32)], [meta, x, w_in, w_out], flops
    )[0]
    pairs_w = [w for pair in zip(w_ins[1:], w_outs[1:], strict=True) for w in pair]
    results = []
    for kind, name in ((1, "mlp_post"), (0, "mlp_pre")):
        near = kind == 1
        results += call(
            functools.partial(mlp_kernel, (kind,), True, near, groups - 1),
            name,
            [(rows3, bf16)] + [((1, row_part, width), bf16)] * near,
            [meta, x, begun, *pairs_w],
            flops * (groups - 1) // 2,
        )
    post, post_near, pre = results

    near = {dy: moved(post, "tile", along_y(-dy)) for dy in (-1, 1)}
    pres = over_mlp(pre)
    far = {0: moved(post_near, "tile", side)}
    for dy in (-1, 1):
        far[dy] = moved(after(post_near, pres[-1]), "tile", both(-dy))
    sizes = (groups, site_rows, depth, heavy, out_scale)
    fixed = [meta, flat_counts, labels]
    grads_own, (query, query_t, *state) = pair_call(
        "pairs_own", [(0, z) for z in z_slots], False, True, False, fixed + [bilinear, *pres], [post] + from_z(post), sizes
    )
    queries = [query, query_t]
    xs = over_mlp(after(x, pres[-1]))
    near = {dy: after(near[dy], state[1]) for dy in (-1, 1)}
    near_z = {dy: from_z(near[dy]) for dy in (-1, 1)}
    grads_near, state = pair_call(
        "pairs_near", [(dy, 0) for dy in (-1, 1)], False, False, False, fixed + queries + state, [near[-1], near[1]], sizes
    )
    far = {dy: after(far[dy], state[1]) for dy in (-1, 0, 1)}
    far_z = {dy: from_z(far[dy]) for dy in (-1, 0, 1)}
    grads_near_z, state = pair_call(
        "pairs_near_z",
        [(dy, z) for dy in (-1, 1) for z in z_slots[1:]],
        False, False, False,
        fixed + queries + state,
        near_z[-1] + near_z[1],
        sizes,
    )
    grads_far, (query_part,) = pair_call(
        "pairs_far",
        [(dy, z) for dy in (-1, 0, 1) for z in z_slots],
        True, False, True,
        fixed + queries + state,
        [one for dy in (-1, 0, 1) for one in [far[dy]] + far_z[dy]],
        sizes,
    )

    def back_from_z(grads):
        return [moved(g, "tile", back_z(slot)) for slot, g in zip(z_slots[1:], grads, strict=True)]

    own_parts = grads_own[:1] + back_from_z(grads_own[1:])
    near_sums = summed(grads_near + back_from_z(grads_near_z), [(0, 2), (2, 2)], bf16, "near_sums")
    near_back = [moved(total, "tile", along_y(dy)) for total, dy in zip(near_sums, (-1, 1), strict=True)]
    query_parts = over_mlp(query_part)
    far_sums = summed(grads_far[:1] + back_from_z(grads_far[1:]), [(0, 1), (1, 1), (2, 1)], bf16, "far_sums")
    far_back = [
        moved(total, "tile", target) for total, target in zip(far_sums, (both(-1), side, both(1)), strict=True)
    ]
    part_t = (groups, 2, hid, row_part)
    active_0, slope_0, active_1, slope_1 = call(
        functools.partial(hidden_kernel, groups),
        "hidden",
        [(part_t, bf16), (part_t, f32)] * 2,
        [meta, w_in, *xs],
        flops * groups // 2,
    )
    in_0, out_0, bil_0, loss = call(
        functools.partial(pre_kernel, groups),
        "pre_grads",
        [((hid, width), f32)] * 2 + [((width, width), f32), ((8, width), f32)],
        [meta, w_out, bilinear, active_0, slope_0, *query_parts, *pres, *xs],
        flops * groups,
        [pltpu.VMEM((2, site_rows, width), bf16)] * 2,
    )
    near_post, far_post = summed(own_parts + near_back, [(0, 1), (1, 1)], f32, "post_sums")
    far_post = over_mlp(far_post.astype(bf16))
    near_post = over_mlp(summed([near_post] + far_back, [(0, 1)], bf16, "near_post")[0])
    half_rows = (2 * hid + width) // 2
    mine, other = call(
        functools.partial(post_kernel, groups),
        "post_grads",
        [((half_rows, width), f32), ((half_rows + 8, width), f32)],
        [meta, w_out, active_1, slope_1, in_0, out_0, bil_0, loss, *near_post, *far_post, *xs],
        flops * groups,
        [pltpu.VMEM((2 * half_rows, width), f32)],
    )

    chips = tile_count // 2
    swap = lambda i: i ^ 1
    same_core = [[core + 2 * chip for chip in range(chips)] for core in range(2)]

    def to_chips(array):
        return lax.all_to_all(array, "tile", 0, 0, tiled=True, axis_index_groups=same_core)

    half_shape, piece = (half_rows, width), (half_rows // chips + 8, width)
    sent, kept = call(
        halves_kernel,
        "halves",
        [(half_shape, bf16), (piece, f32)],
        [meta, mine, moved(other, "tile", swap), loss],
        scratch=[pltpu.VMEM(half_shape, f32)],
    )
    joined_shape = (half_rows + 8 * chips, width)
    total = call(total_kernel, "total", [(joined_shape, f32)], [meta, to_chips(sent), kept])[0]
    joined = to_chips(total)
    share = 1.0 / (2.0 * tile_count * site_rows * 27 * site_rows)
    grad_in, grad_out, grad_bilinear, pair_loss = call(
        functools.partial(last_kernel, chips, share),
        "last",
        [((width, hid), f32), ((hid, width), f32), ((width, width), f32), ((8, 128), f32)],
        [meta, joined, moved(joined, "tile", swap)],
        scratch=[pltpu.VMEM((2 * half_rows, width), f32)],
    )
    return (pair_loss[0, 0], grad_in, grad_out, grad_bilinear)


def solution(mesh):
    placed = (P("tile", "mlp", None, None, None), P(None, "mlp"), P("mlp", None), P(), P(), P())
    return jax.shard_map(
        local,
        mesh=mesh,
        in_specs=placed,
        out_specs=(P(), P(None, "mlp"), P("mlp", None), P()),
        check_vma=False,
    )
```

```python
import functools

import jax
import jax.numpy as jnp
from jax import lax
from jax.experimental import pallas as pl
from jax.experimental.pallas import tpu as pltpu
from jax.sharding import PartitionSpec as P

f32 = jnp.float32
bf16 = jnp.bfloat16
OFF = -1e30
VMEM = pl.BlockSpec(memory_space=pltpu.VMEM)
SMEM = pl.BlockSpec(memory_space=pltpu.SMEM)


def dot(a, b):
    return lax.dot_general(a, b, (((1,), (0,)), ((), ())), preferred_element_type=f32)


def moved(array, axis, target):
    peers = lax.axis_size(axis)
    pairs = [(i, target(i)) for i in range(peers) if target(i) is not None]
    return lax.ppermute(array, axis, pairs)


def over_mlp(array):
    groups = lax.axis_size("mlp")
    if groups == 2:
        return [array, moved(array, "mlp", lambda i: 1 - i)]
    gathered = lax.all_gather(array, "mlp", axis=0)
    member = lax.axis_index("mlp")
    order = [lax.rem(member + step, groups) for step in range(groups)]
    return [lax.dynamic_index_in_dim(gathered, g, 0, keepdims=False) for g in order]


def owner(meta, step, groups):
    return lax.rem(meta[1] + step, groups)


def call(kernel, name, outs, operands, flops=0, scratch=(), aliases=None):
    specs = [SMEM if o.dtype == jnp.int32 and o.ndim == 1 else VMEM for o in operands]
    size = sum(o.size * o.dtype.itemsize for o in operands)
    return pl.pallas_call(
        kernel,
        out_shape=[jax.ShapeDtypeStruct(shape, kind) for shape, kind in outs],
        in_specs=specs,
        out_specs=[VMEM] * len(outs),
        scratch_shapes=list(scratch),
        input_output_aliases=aliases or {},
        compiler_params=pltpu.CompilerParams(vmem_limit_bytes=40 * 1024 * 1024),
        cost_estimate=pl.CostEstimate(flops=flops, bytes_accessed=size, transcendentals=0),
        name=name,
    )(*operands)


def summed(arrays, places, kind, name):
    def kernel(*refs):
        for (first, count), out in zip(places, refs[len(arrays) :], strict=True):
            for t in range(count):
                total = None
                for ref in refs[: len(arrays)]:
                    if first + t < ref.shape[0]:
                        part = ref[first + t].astype(f32)
                        total = part if total is None else total + part
                out[t] = total.astype(kind)

    shape = arrays[0].shape[1:]
    return call(kernel, name, [((count, *shape), kind) for unused, count in places], arrays)


def sub_tile(xb, t):
    return 1 - xb if t == 0 else xb


def gelu_parts(h):
    c = 0.7978845608028654
    square = h * h
    bend = jnp.tanh(c * (h + 0.044715 * (square * h)))
    whole = 0.5 * (1.0 + bend)
    slope = whole + 0.5 * h * (1.0 - bend * bend) * (c * (1.0 + 3 * 0.044715 * square))
    return h * whole, slope


def mlp_own_kernel(meta, x0_ref, x1_ref, w_in_ref, w_out_ref, sum0_ref, sum1_ref):
    for x_ref, out_ref in ((x1_ref, sum1_ref), (x0_ref, sum0_ref)):
        for t in range(2):
            hidden = dot(x_ref[sub_tile(meta[2], t)], w_in_ref[...])
            out_ref[t] = dot(gelu_parts(hidden)[0].astype(bf16), w_out_ref[...])


def mlp_kernel(begun, groups, meta, x_ref, *refs):
    refs = list(refs)
    start_ref = refs.pop(0) if begun else None
    outs = refs[2 * groups :]
    for t in range(2):
        x = x_ref[sub_tile(meta[2], t)]
        total = start_ref[t] if begun else None
        for g in range(groups):
            hidden = dot(x, refs[2 * g][...])
            part = dot(gelu_parts(hidden)[0].astype(bf16), refs[2 * g + 1][...])
            total = part if total is None else total + part
        embedded = (x.astype(f32) + total).astype(bf16)
        outs[0][t] = embedded
        if t == 0 and len(outs) == 2:
            outs[1][0] = embedded


def hidden_kernel(groups, meta, w_in_ref, *refs):
    w_t = w_in_ref[...].T
    outs = refs[2 * groups :]
    for kind in range(2):
        for g in range(groups):
            for u in range(2):
                active, slope = gelu_parts(dot(w_t, refs[kind * groups + g][u].T))
                outs[2 * kind][g, u] = active.astype(bf16)
                outs[2 * kind + 1][g, u] = slope


def weight_part(back, x, active_t, slope_t, w_out, sums):
    active_grad = dot(w_out, back.T)
    hidden_grad = (active_grad * slope_t).astype(bf16)
    return sums[0] + dot(hidden_grad, x), sums[1] + dot(active_t, back)


def pre_kernel(groups, meta, w_out_ref, bil_ref, active_ref, slope_ref, *refs):
    query_refs, pre_refs, x_refs = refs[:groups], refs[groups : 2 * groups], refs[2 * groups : 3 * groups]
    in_ref, out_ref, bil_grad_ref, loss_ref, pre_all, back_all = refs[3 * groups :]
    rows = pre_refs[0].shape[1]
    site_rows = rows * groups
    xb = meta[2]
    bil_t = bil_ref[...].T
    bil_grad = jnp.zeros(bil_grad_ref.shape, f32)
    sums = (jnp.zeros(in_ref.shape, f32), jnp.zeros(out_ref.shape, f32))
    for a in range(2):
        total = query_refs[0][a * site_rows : (a + 1) * site_rows]
        for ref in query_refs[1:]:
            total = total + ref[a * site_rows : (a + 1) * site_rows]
        query_back = total.astype(bf16)
        for g in range(groups):
            place = pl.ds(pl.multiple_of(owner(meta, g, groups) * rows, rows), rows)
            pre_all[a, place, :] = pre_refs[g][a]
        for g in range(groups):
            place = slice(g * rows, (g + 1) * rows)
            bil_grad = bil_grad + dot(pre_all[a, place, :].T, query_back[place])
        back_all[a] = dot(query_back, bil_t).astype(bf16)
        u = sub_tile(xb, a)
        for g in range(groups):
            place = pl.ds(pl.multiple_of(owner(meta, g, groups) * rows, rows), rows)
            back = back_all[a, place, :]
            sums = weight_part(back, x_refs[g][u], active_ref[g, u], slope_ref[g, u], w_out_ref[...], sums)
    in_ref[...], out_ref[...] = sums
    bil_grad_ref[...] = bil_grad
    loss = query_refs[0][2 * site_rows :]
    for ref in query_refs[1:]:
        loss = loss + ref[2 * site_rows :]
    loss_ref[...] = loss


def post_kernel(groups, meta, w_out_ref, active_ref, slope_ref, in0, out0, bil0, loss0, *refs):
    near_refs, far_refs, x_refs = refs[:groups], refs[groups : 2 * groups], refs[2 * groups : 3 * groups]
    mine_ref, other_ref, whole = refs[3 * groups :]
    xb = meta[2]
    core = lax.rem(meta[0], 2)
    sums = (in0[...], out0[...])
    for t in range(2):
        u = sub_tile(xb, t)
        for g in range(groups):
            back = (near_refs, far_refs)[t][g][0]
            sums = weight_part(back, x_refs[g][u], active_ref[g, u], slope_ref[g, u], w_out_ref[...], sums)
    hid = in0.shape[0]
    half = mine_ref.shape[0]
    whole[:hid] = sums[0]
    whole[hid : 2 * hid] = sums[1]
    whole[2 * hid :] = bil0[...]
    mine_ref[...] = whole[pl.ds(pl.multiple_of(core * half, 16), half), :]
    other_ref[:half] = whole[pl.ds(pl.multiple_of((1 - core) * half, 16), half), :]
    other_ref[half:] = loss0[...]


def halves_kernel(meta, mine_ref, other_ref, loss0, sent_ref, kept_ref, whole):
    rows = kept_ref.shape[0] - 8
    half = mine_ref.shape[0]
    whole[...] = mine_ref[...] + other_ref[:half]
    sent_ref[...] = whole[...].astype(sent_ref.dtype)
    kept_ref[rows:] = loss0[...] + other_ref[half:]
    kept_ref[:rows] = whole[pl.ds(pl.multiple_of(meta[0] // 2 * rows, 16), rows), :]


def exponent(largest):
    return 14.0 - jnp.ceil(jnp.log2(jnp.maximum(largest, 1e-30)))


def total_kernel(meta, got_ref, kept_ref, out_ref, coded):
    rows = kept_ref.shape[0] - 8
    chips = got_ref.shape[0] // rows
    total = kept_ref[:rows]
    for n in range(chips):
        piece = got_ref[n * rows : (n + 1) * rows, :].astype(f32)
        total = total + jnp.where(n == meta[0] // 2, 0.0, piece)
    width = total.shape[1]
    line = lax.broadcasted_iota(jnp.int32, (16, width), 0)
    notes = jnp.zeros((16, width), f32)
    for k in range(rows // 16):
        part = total[k * 16 : (k + 1) * 16]
        power = exponent(jnp.max(jnp.max(jnp.abs(part), 0, keepdims=True), 1, keepdims=True))
        coded[k * 16 : (k + 1) * 16, :] = jnp.round(part * jnp.exp2(power)).astype(jnp.int32).astype(jnp.int16)
        notes = jnp.where(line == k, power, notes)
    loss = kept_ref[rows : rows + 1]
    power = exponent(jnp.max(loss, 1, keepdims=True))
    scaled = loss * jnp.exp2(power)
    high = jnp.floor(scaled)
    low = jnp.floor((scaled - high) * 16384.0)
    for k, note in ((13, power), (14, high), (15, low)):
        notes = jnp.where(line == k, note, notes)
    coded[rows:, :] = notes.astype(jnp.int32).astype(jnp.int16)
    for n in range(chips):
        out_ref[n * (rows + 16) : (n + 1) * (rows + 16), :] = coded[...]


def last_kernel(chips, share, meta, mine_ref, other_ref, in_ref, out_ref, bil_ref, loss_ref, whole):
    core = lax.rem(meta[0], 2)
    half = whole.shape[0] // 2
    rows = half // chips
    loss = jnp.zeros((1, 128), f32)
    for n in range(chips):
        first = n * (rows + 16)
        for ref, side in ((mine_ref, core), (other_ref, 1 - core)):
            piece = ref[first : first + rows + 16, :].astype(jnp.int32).astype(f32)
            notes = piece[rows:]
            for k in range(rows // 16):
                place = side * half + n * rows + k * 16
                part = piece[k * 16 : (k + 1) * 16] * jnp.exp2(-notes[k : k + 1])
                whole[pl.ds(pl.multiple_of(place, 16), 16), :] = part
            if ref is mine_ref:
                loss = loss + (notes[14:15] + notes[15:16] / 16384.0)[:, :128] * jnp.exp2(-notes[13:14, :128])
    hid = out_ref.shape[0]
    in_ref[...] = whole[:hid].T
    out_ref[...] = whole[hid : 2 * hid]
    bil_ref[...] = whole[2 * hid :]
    loss_ref[...] = jnp.broadcast_to(loss * share, loss_ref.shape)


def pair_kernel(slots, foreign, first, last, groups, site_rows, depth, heavy, out_scale, *refs):
    refs = list(refs)

    def take(count):
        taken = refs[:count]
        del refs[:count]
        return taken

    meta, counts, label_ref = take(3)
    if first:
        bil_ref = take(1)[0]
        pre_refs = take(groups)
    else:
        q_ref, qt_ref, acc_in, loss_in, hit_in, found_in = take(6)
    post_refs = take(len(slots))
    z_list = list(dict.fromkeys(z for unused, z in slots))
    grad_refs = dict(zip(z_list, take(len(z_list)), strict=True))
    if first:
        q_ref, qt_ref = take(2)
    if last:
        out_ref, acc, loss_ref, hit_ref, found_ref = refs
    else:
        acc, loss_ref, hit_ref, found_ref = refs
    tile_here, member, xb = meta[0], meta[1], meta[2]
    yg = lax.rem(tile_here // depth, 4)
    zg = lax.rem(tile_here, depth)
    toward = 1 - 2 * xb
    rows = post_refs[0].shape[1]
    width = post_refs[0].shape[2]
    if first:
        scale = jnp.asarray(width ** (-0.5), bf16)
        for a in range(2):
            for g in range(groups):
                part = dot(pre_refs[g][a], bil_ref[...]).astype(bf16)
                place = pl.ds(pl.multiple_of(owner(meta, g, groups) * rows, rows), rows)
                q_ref[a, place, :] = part
            qt_ref[a] = (q_ref[a] * scale).T
        acc[...] = jnp.zeros_like(acc)
        loss_ref[...] = jnp.zeros_like(loss_ref)
        hit_ref[...] = jnp.zeros_like(hit_ref)
        found_ref[...] = jnp.zeros_like(found_ref)
    elif last:
        acc[...] = acc_in[...]
        loss_ref[...] = loss_in[...]
        hit_ref[...] = hit_in[...]
        found_ref[...] = found_in[...]
    j_own = lax.broadcasted_iota(jnp.int32, (rows, site_rows), 0)
    j_col = lax.broadcasted_iota(jnp.int32, (rows, 128), 0)
    i_row = lax.broadcasted_iota(jnp.int32, (1, site_rows), 1)
    step = rows // (8 if rows >= 128 else 4)
    i_ok = [i_row < counts[tile_here * 4 + sub_tile(xb, a) * 2] for a in (0, 1)]
    i_bias = [jnp.where(ok, 0.0, OFF).astype(f32) for ok in i_ok]
    if foreign:
        nz = sum(1 for dy, unused in slots if dy == 0)
        chunks = [[(n, 0) for n in range(k, k + nz)] for k in range(0, len(slots), nz)]
    else:
        chunks = [[(n, 0), (n, 1)] for n in range(len(slots))]
    for chunk in chunks:
        post = jnp.concatenate([post_refs[n][t] for n, t in chunk], 0)
        post_t = post.T
        places = []
        for n, t in chunk:
            sign, z_slot = slots[n]
            dy = sign * (1 - 2 * lax.rem(yg, 2))
            if depth == 2:
                z_other = zg if z_slot == 0 else 1 - zg
            else:
                z_other = zg + z_slot
            x_other = 1 - xb if foreign else xb
            y_other = yg + dy
            inside = (y_other >= 0) & (y_other < 4) & (z_other >= 0) & (z_other < depth)
            source = jnp.where(inside, x_other * 4 * depth + y_other * depth + z_other, tile_here)
            valid = jnp.clip(counts[source * 4 + sub_tile(x_other, t) * 2 + 1] - member * rows, 0, rows)
            places.append((t, dy, z_other - zg, jnp.where(inside, valid, 0)))
        j_bias = jnp.concatenate([jnp.where(j_col < place[3], 0.0, OFF).astype(f32) for place in places], 0)
        j_bias = jnp.concatenate([j_bias] * (site_rows // 128), 1)
        total = None
        for a in (0,) if foreign else (0, 1):
            targets = []
            for t, dy, dz, valid in places:
                dx = toward if foreign else 0 if t == a else -toward if a == 0 else toward
                base = ((dx + 1) * 9 + (dy + 1) * 3 + dz + 1) * site_rows + member * rows
                key = label_ref[sub_tile(xb, a)] - base
                key = jnp.where(i_ok[a] & (key < valid), key, -1)
                found_ref[a] += jnp.where(key >= 0, 1.0, 0.0)
                targets.append(j_own == key)
            target = jnp.concatenate(targets, 0)
            s = dot(post, qt_ref[a]) + j_bias + i_bias[a]
            e = jnp.exp(-jnp.abs(s))
            w = 1.0 + e
            r = pl.reciprocal(w, approx=True)
            chance = jnp.where(s >= 0.0, r, e * r)
            slope = jnp.where(target, (chance - 1.0) * heavy, chance).astype(bf16)
            part = dot(slope, q_ref[a])
            total = part if total is None else total + part
            acc[a] += dot(post_t, slope)
            piece = hit = None
            for k in range(len(chunk)):
                product = small = above = None
                for g in range(k * rows, (k + 1) * rows, step):
                    here = slice(g, g + step)
                    more = jnp.maximum(s[here], 0.0)
                    found = jnp.where(target[here], s[here], 0.0)
                    product = w[here] if product is None else product * w[here]
                    small = e[here] if small is None else small + e[here]
                    above = more if above is None else above + more
                    hit = found if hit is None else hit + found
                loss = above + jnp.where(small < 1e-3, small, jnp.log(product))
                piece = loss if piece is None else piece + loss
            loss_ref[...] += jnp.sum(piece.reshape(step // 8, 8, site_rows), 0)
            hit_ref[a] += jnp.sum(hit.reshape(step // 8, 8, site_rows), 0)
        for k, (n, t) in enumerate(chunk):
            dy, z_slot = slots[n]
            place = [other for other, z in slots if z == z_slot].index(dy) * post_refs[n].shape[0] + t
            grad_refs[z_slot][place] = total[k * rows : (k + 1) * rows] * out_scale
    if last:
        total = jnp.sum(loss_ref[...])
        for a in range(2):
            out_ref[a * site_rows : (a + 1) * site_rows] = (acc[a] * out_scale).T
            score = jnp.sum(hit_ref[a], 0, keepdims=True)
            soft = jnp.log1p(jnp.exp(-jnp.abs(score)))
            missed = heavy * (jnp.maximum(-score, 0.0) + soft) - (jnp.maximum(score, 0.0) + soft)
            total = total + jnp.sum(jnp.where(found_ref[a] > 0.0, missed, 0.0))
        out_ref[2 * site_rows :] = jnp.full((8, width), total, f32)


def pair_call(name, slots, foreign, first, last, operands, posts, sizes):
    tiles, rows, width = posts[0].shape
    groups, site_rows = sizes[0], sizes[1]
    kernel = functools.partial(pair_kernel, slots, foreign, first, last, *sizes)
    state = [
        ((2, width, site_rows), f32),
        ((8, site_rows), f32),
        ((2, 8, site_rows), f32),
        ((2, 1, site_rows), f32),
    ]
    z_count = len(set(z for unused, z in slots))
    outs = [((tiles * len(slots) // z_count, rows, width), f32)] * z_count
    if first:
        outs += [((2, site_rows, width), bf16), ((2, width, site_rows), bf16)]
    if last:
        outs += [((2 * site_rows + 8, width), f32)]
    else:
        outs += state
    pairs = len(slots) * (1 if foreign else 4)
    aliases = {} if first or last else {5 + n: z_count + n for n in range(4)}
    results = call(
        kernel,
        name,
        outs,
        operands + posts,
        flops=pairs * rows * site_rows * width * 40,
        scratch=[pltpu.VMEM(shape, kind) for shape, kind in state] if last else (),
        aliases=aliases,
    )
    return list(results[:z_count]), list(results[z_count:])


def after(array, *others):
    return lax.optimization_barrier((array, *others))[0]


def local(features, w_in, w_out, bilinear, partner, counts):
    row_part = features.shape[1]
    width = features.shape[4]
    hid = w_in.shape[1]
    groups = lax.axis_size("mlp")
    site_rows = row_part * groups
    tile_count = lax.axis_size("tile")
    depth = tile_count // 8
    tile_here = lax.axis_index("tile")
    member = lax.axis_index("mlp")
    xb = tile_here // (4 * depth)
    heavy = float(27 * site_rows // 4)
    out_scale = width ** (-0.5) / (2 * tile_count * site_rows)
    half = tile_count // 2

    def side(i):
        return i ^ half

    def along_y(sign):
        def target(i):
            y = i // depth % 4
            step = sign * (1 - 2 * (y % 2))
            return i + step * depth if 0 <= y + step < 4 else None

        return target

    def both(sign):
        return lambda i: None if along_y(sign)(i) is None else along_y(sign)(i) ^ half

    z_slots = (0, 1) if depth == 2 else (0, -1, 1)

    def along_z(slot):
        if depth == 2:
            return lambda i: i ^ 1
        return lambda i: i - slot if 0 <= i % depth - slot < depth else None

    def back_z(slot):
        return along_z(slot if depth == 2 else -slot)

    def from_z(array):
        return [moved(array, "tile", along_z(slot)) for slot in z_slots[1:]]

    w_ins, w_outs = over_mlp(w_in), over_mlp(w_out)
    meta = jnp.stack([tile_here, member, xb]).astype(jnp.int32)
    x0, x1 = [jnp.transpose(features[0, :, :, kind], (1, 0, 2)) for kind in (0, 1)]
    x0s, x1s = over_mlp(x0), over_mlp(x1)
    labels = lax.dynamic_index_in_dim(partner, tile_here, 0, keepdims=False)[:, None, :]
    flat_counts = counts.reshape(-1)
    rows3 = (2, row_part, width)
    flops = 4 * row_part * width * hid * 4
    begun = call(mlp_own_kernel, "mlp_own", [(rows3, f32)] * 2, [meta, x0, x1, w_in, w_out], flops)
    pairs_w = [w for pair in zip(w_ins[1:], w_outs[1:], strict=True) for w in pair]
    more = functools.partial(mlp_kernel, True, groups - 1)
    near_shape = (1, row_part, width)
    post, post_near = call(
        more, "mlp_post", [(rows3, bf16), (near_shape, bf16)], [meta, x1, begun[1], *pairs_w], flops * (groups - 1) // 2
    )
    pre = call(more, "mlp_pre", [(rows3, bf16)], [meta, x0, begun[0], *pairs_w], flops * (groups - 1) // 2)[0]
    if groups == 2:
        full = functools.partial(mlp_kernel, False, 2)
        pres = [pre, call(full, "mlp_pre_other", [(rows3, bf16)], [meta, x0s[1], w_in, w_out, *pairs_w], flops)[0]]
    else:
        pres = over_mlp(pre)

    near = {dy: moved(post, "tile", along_y(dy)) for dy in (-1, 1)}
    far = {0: moved(post_near, "tile", side)}
    sizes = (groups, site_rows, depth, heavy, out_scale)
    fixed = [meta, flat_counts, labels]
    grads_own, (query, query_t, *state) = pair_call(
        "pairs_own", [(0, z) for z in z_slots], False, True, False, fixed + [bilinear, *pres], [post] + from_z(post), sizes
    )
    queries = [query, query_t]
    for dy in (-1, 1):
        far[dy] = moved(after(post_near, state[1]), "tile", both(dy))
    near = {dy: after(near[dy], state[1], x1s[-1]) for dy in (-1, 1)}
    near_z = {dy: from_z(near[dy]) for dy in (-1, 1)}
    grads_near, state = pair_call(
        "pairs_near", [(dy, 0) for dy in (-1, 1)], False, False, False, fixed + queries + state, [near[-1], near[1]], sizes
    )
    far = {dy: after(far[dy], state[1]) for dy in (-1, 0, 1)}
    far_z = {dy: from_z(far[dy]) for dy in (-1, 0, 1)}
    grads_near_z, state = pair_call(
        "pairs_near_z",
        [(dy, z) for dy in (-1, 1) for z in z_slots[1:]],
        False, False, False,
        fixed + queries + state,
        near_z[-1] + near_z[1],
        sizes,
    )
    grads_far, (query_part,) = pair_call(
        "pairs_far",
        [(dy, z) for dy in (-1, 0, 1) for z in z_slots],
        True, False, True,
        fixed + queries + state,
        [one for dy in (-1, 0, 1) for one in [far[dy]] + far_z[dy]],
        sizes,
    )

    def back_from_z(grads):
        return [moved(g, "tile", back_z(slot)) for slot, g in zip(z_slots[1:], grads, strict=True)]

    own_parts = grads_own[:1] + back_from_z(grads_own[1:])
    near_sums = summed(grads_near + back_from_z(grads_near_z), [(0, 2), (2, 2)], bf16, "near_sums")
    near_back = [moved(total, "tile", along_y(dy)) for total, dy in zip(near_sums, (-1, 1), strict=True)]
    query_parts = over_mlp(query_part)
    far_sums = summed(grads_far[:1] + back_from_z(grads_far[1:]), [(0, 1), (1, 1), (2, 1)], bf16, "far_sums")
    far_back = [moved(far_sums[0], "tile", both(-1)), moved(far_sums[2], "tile", both(1))]
    far_back.append(moved(after(far_sums[1], near_back[0]), "tile", side))
    part_t = (groups, 2, hid, row_part)
    active_0, slope_0, active_1, slope_1 = call(
        functools.partial(hidden_kernel, groups),
        "hidden",
        [(part_t, bf16), (part_t, f32)] * 2,
        [meta, w_in, *x0s, *x1s],
        flops * groups // 2,
    )
    in_0, out_0, bil_0, loss = call(
        functools.partial(pre_kernel, groups),
        "pre_grads",
        [((hid, width), f32)] * 2 + [((width, width), f32), ((8, width), f32)],
        [meta, w_out, bilinear, active_0, slope_0, *query_parts, *pres, *x0s],
        flops * groups,
        [pltpu.VMEM((2, site_rows, width), bf16)] * 2,
    )
    near_post, far_post = summed(own_parts + near_back, [(0, 1), (1, 1)], f32, "post_sums")
    far_post = over_mlp(far_post.astype(bf16))
    near_post = over_mlp(summed([near_post] + far_back, [(0, 1)], bf16, "near_post")[0])
    half_rows = (2 * hid + width) // 2
    mine, other = call(
        functools.partial(post_kernel, groups),
        "post_grads",
        [((half_rows, width), f32), ((half_rows + 8, width), f32)],
        [meta, w_out, active_1, slope_1, in_0, out_0, bil_0, loss, *near_post, *far_post, *x1s],
        flops * groups,
        [pltpu.VMEM((2 * half_rows, width), f32)],
    )

    chips = tile_count // 2
    swap = lambda i: i ^ 1
    same_core = [[core + 2 * chip for chip in range(chips)] for core in range(2)]

    def to_chips(array):
        return lax.all_to_all(array, "tile", 0, 0, tiled=True, axis_index_groups=same_core)

    half_shape, piece = (half_rows, width), (half_rows // chips + 8, width)
    sent, kept = call(
        halves_kernel,
        "halves",
        [(half_shape, bf16), (piece, f32)],
        [meta, mine, moved(other, "tile", swap), loss],
        scratch=[pltpu.VMEM(half_shape, f32)],
    )
    coded = (half_rows // chips + 16, width)
    total = call(
        total_kernel,
        "total",
        [((chips * coded[0], width), jnp.int16)],
        [meta, to_chips(sent), kept],
        scratch=[pltpu.VMEM(coded, jnp.int16)],
    )[0]
    joined = to_chips(total)
    share = 1.0 / (2.0 * tile_count * site_rows * 27 * site_rows)
    grad_in, grad_out, grad_bilinear, pair_loss = call(
        functools.partial(last_kernel, chips, share),
        "last",
        [((width, hid), f32), ((hid, width), f32), ((width, width), f32), ((8, 128), f32)],
        [meta, joined, moved(joined, "tile", swap)],
        scratch=[pltpu.VMEM((2 * half_rows, width), f32)],
    )
    return (pair_loss[0, 0], grad_in, grad_out, grad_bilinear)


def solution(mesh):
    placed = (P("tile", "mlp", None, None, None), P(None, "mlp"), P("mlp", None), P(), P(), P())
    return jax.shard_map(
        local,
        mesh=mesh,
        in_specs=placed,
        out_specs=(P(), P(None, "mlp"), P("mlp", None), P()),
        check_vma=False,
    )
```

```python
import functools

import jax
import jax.numpy as jnp
from jax import lax
from jax.experimental import pallas as pl
from jax.experimental.pallas import tpu as pltpu
from jax.sharding import PartitionSpec as P

f32 = jnp.float32
bf16 = jnp.bfloat16
OFF = -1e30
VMEM = pl.BlockSpec(memory_space=pltpu.VMEM)
SMEM = pl.BlockSpec(memory_space=pltpu.SMEM)


def dot(a, b):
    return lax.dot_general(a, b, (((1,), (0,)), ((), ())), preferred_element_type=f32)


def moved(array, axis, target):
    peers = lax.axis_size(axis)
    pairs = [(i, target(i)) for i in range(peers) if target(i) is not None]
    return lax.ppermute(array, axis, pairs)


def over_mlp(array):
    groups = lax.axis_size("mlp")
    if groups == 2:
        return [array, moved(array, "mlp", lambda i: 1 - i)]
    gathered = lax.all_gather(array, "mlp", axis=0)
    member = lax.axis_index("mlp")
    order = [lax.rem(member + step, groups) for step in range(groups)]
    return [lax.dynamic_index_in_dim(gathered, g, 0, keepdims=False) for g in order]


def owner(meta, step, groups):
    return lax.rem(meta[1] + step, groups)


def call(kernel, name, outs, operands, flops=0, scratch=(), aliases=None):
    specs = [SMEM if o.dtype == jnp.int32 and o.ndim == 1 else VMEM for o in operands]
    size = sum(o.size * o.dtype.itemsize for o in operands)
    return pl.pallas_call(
        kernel,
        out_shape=[jax.ShapeDtypeStruct(shape, kind) for shape, kind in outs],
        in_specs=specs,
        out_specs=[VMEM] * len(outs),
        scratch_shapes=list(scratch),
        input_output_aliases=aliases or {},
        compiler_params=pltpu.CompilerParams(vmem_limit_bytes=40 * 1024 * 1024),
        cost_estimate=pl.CostEstimate(flops=flops, bytes_accessed=size, transcendentals=0),
        name=name,
    )(*operands)


def summed(arrays, places, name):
    def kernel(*refs):
        for (first, count, kind), out in zip(places, refs[len(arrays) :], strict=True):
            for t in range(count):
                total = None
                for ref in refs[: len(arrays)]:
                    if first + t < ref.shape[0]:
                        part = ref[first + t].astype(f32)
                        total = part if total is None else total + part
                out[t] = total.astype(kind)

    shape = arrays[0].shape[1:]
    return call(kernel, name, [((count, *shape), kind) for unused, count, kind in places], arrays)


def sub_tile(xb, t):
    return 1 - xb if t == 0 else xb


def gelu_parts(h):
    c = 0.7978845608028654
    square = h * h
    bend = jnp.tanh(c * (h + 0.044715 * (square * h)))
    whole = 0.5 * (1.0 + bend)
    slope = whole + 0.5 * h * (1.0 - bend * bend) * (c * (1.0 + 3 * 0.044715 * square))
    return h * whole, slope


def mlp_own_kernel(meta, x0_ref, x1_ref, w_in_ref, w_out_ref, sum0_ref, sum1_ref):
    for x_ref, out_ref in ((x1_ref, sum1_ref), (x0_ref, sum0_ref)):
        for t in range(2):
            hidden = dot(x_ref[sub_tile(meta[2], t)], w_in_ref[...])
            out_ref[t] = dot(gelu_parts(hidden)[0].astype(bf16), w_out_ref[...])


def mlp_kernel(begun, groups, meta, x_ref, *refs):
    refs = list(refs)
    start_ref = refs.pop(0) if begun else None
    outs = refs[2 * groups :]
    for t in range(2):
        x = x_ref[sub_tile(meta[2], t)]
        total = start_ref[t] if begun else None
        for g in range(groups):
            hidden = dot(x, refs[2 * g][...])
            part = dot(gelu_parts(hidden)[0].astype(bf16), refs[2 * g + 1][...])
            total = part if total is None else total + part
        embedded = (x.astype(f32) + total).astype(bf16)
        outs[0][t] = embedded
        if t == 0 and len(outs) == 2:
            outs[1][0] = embedded


def hidden_kernel(groups, meta, w_in_ref, *refs):
    w_t = w_in_ref[...].T
    outs = refs[2 * groups :]
    for kind in range(2):
        for g in range(groups):
            for u in range(2):
                active, slope = gelu_parts(dot(w_t, refs[kind * groups + g][u].T))
                outs[2 * kind][g, u] = active.astype(bf16)
                outs[2 * kind + 1][g, u] = slope


def weight_part(back, x, active_t, slope_t, w_out, sums):
    active_grad = dot(w_out, back.T)
    hidden_grad = (active_grad * slope_t).astype(bf16)
    return sums[0] + dot(hidden_grad, x), sums[1] + dot(active_t, back)


def pre_kernel(groups, meta, w_out_ref, bil_ref, active_ref, slope_ref, *refs):
    query_refs, pre_refs, x_refs = refs[:groups], refs[groups : 2 * groups], refs[2 * groups : 3 * groups]
    in_ref, out_ref, bil_grad_ref, loss_ref, pre_all, back_all = refs[3 * groups :]
    rows = pre_refs[0].shape[1]
    site_rows = rows * groups
    xb = meta[2]
    bil_t = bil_ref[...].T
    bil_grad = jnp.zeros(bil_grad_ref.shape, f32)
    sums = (jnp.zeros(in_ref.shape, f32), jnp.zeros(out_ref.shape, f32))
    for a in range(2):
        total = query_refs[0][a * site_rows : (a + 1) * site_rows]
        for ref in query_refs[1:]:
            total = total + ref[a * site_rows : (a + 1) * site_rows]
        query_back = total.astype(bf16)
        for g in range(groups):
            place = pl.ds(pl.multiple_of(owner(meta, g, groups) * rows, rows), rows)
            pre_all[a, place, :] = pre_refs[g][a]
        for g in range(groups):
            place = slice(g * rows, (g + 1) * rows)
            bil_grad = bil_grad + dot(pre_all[a, place, :].T, query_back[place])
        back_all[a] = dot(query_back, bil_t).astype(bf16)
        u = sub_tile(xb, a)
        for g in range(groups):
            place = pl.ds(pl.multiple_of(owner(meta, g, groups) * rows, rows), rows)
            back = back_all[a, place, :]
            sums = weight_part(back, x_refs[g][u], active_ref[g, u], slope_ref[g, u], w_out_ref[...], sums)
    in_ref[...], out_ref[...] = sums
    bil_grad_ref[...] = bil_grad
    loss = query_refs[0][2 * site_rows :]
    for ref in query_refs[1:]:
        loss = loss + ref[2 * site_rows :]
    loss_ref[...] = loss


def post_kernel(groups, meta, w_out_ref, active_ref, slope_ref, in0, out0, bil0, loss0, *refs):
    back_refs, x_refs = refs[:groups], refs[groups : 2 * groups]
    mine_ref, other_ref, whole = refs[2 * groups :]
    xb = meta[2]
    core = lax.rem(meta[0], 2)
    sums = (in0[...], out0[...])
    for t in range(2):
        u = sub_tile(xb, t)
        for g in range(groups):
            back = back_refs[g][t]
            sums = weight_part(back, x_refs[g][u], active_ref[g, u], slope_ref[g, u], w_out_ref[...], sums)
    hid = in0.shape[0]
    half = mine_ref.shape[0]
    whole[:hid] = sums[0]
    whole[hid : 2 * hid] = sums[1]
    whole[2 * hid :] = bil0[...]
    mine_ref[...] = whole[pl.ds(pl.multiple_of(core * half, 16), half), :]
    other_ref[:half] = whole[pl.ds(pl.multiple_of((1 - core) * half, 16), half), :]
    other_ref[half:] = loss0[...]


def halves_kernel(meta, mine_ref, other_ref, loss0, sent_ref, kept_ref, whole):
    rows = kept_ref.shape[0] - 8
    half = mine_ref.shape[0]
    whole[...] = mine_ref[...] + other_ref[:half]
    sent_ref[...] = whole[...].astype(sent_ref.dtype)
    kept_ref[rows:] = loss0[...] + other_ref[half:]
    kept_ref[:rows] = whole[pl.ds(pl.multiple_of(meta[0] // 2 * rows, 16), rows), :]


def exponent(largest):
    return 14.0 - jnp.ceil(jnp.log2(jnp.maximum(largest, 1e-30)))


def total_kernel(meta, got_ref, kept_ref, out_ref, coded):
    rows = kept_ref.shape[0] - 8
    chips = got_ref.shape[0] // rows
    total = kept_ref[:rows]
    for n in range(chips):
        piece = got_ref[n * rows : (n + 1) * rows, :].astype(f32)
        total = total + jnp.where(n == meta[0] // 2, 0.0, piece)
    width = total.shape[1]
    line = lax.broadcasted_iota(jnp.int32, (16, width), 0)
    notes = jnp.zeros((16, width), f32)
    for k in range(rows // 16):
        part = total[k * 16 : (k + 1) * 16]
        power = exponent(jnp.max(jnp.max(jnp.abs(part), 0, keepdims=True), 1, keepdims=True))
        coded[k * 16 : (k + 1) * 16, :] = jnp.round(part * jnp.exp2(power)).astype(jnp.int32).astype(jnp.int16)
        notes = jnp.where(line == k, power, notes)
    loss = kept_ref[rows : rows + 1]
    power = exponent(jnp.max(loss, 1, keepdims=True))
    scaled = loss * jnp.exp2(power)
    high = jnp.floor(scaled)
    low = jnp.floor((scaled - high) * 16384.0)
    for k, note in ((13, power), (14, high), (15, low)):
        notes = jnp.where(line == k, note, notes)
    coded[rows:, :] = notes.astype(jnp.int32).astype(jnp.int16)
    for n in range(chips):
        out_ref[n * (rows + 16) : (n + 1) * (rows + 16), :] = coded[...]


def last_kernel(chips, share, meta, mine_ref, other_ref, in_ref, out_ref, bil_ref, loss_ref, whole):
    core = lax.rem(meta[0], 2)
    half = whole.shape[0] // 2
    rows = half // chips
    loss = jnp.zeros((1, 128), f32)
    for n in range(chips):
        first = n * (rows + 16)
        for ref, side in ((mine_ref, core), (other_ref, 1 - core)):
            piece = ref[first : first + rows + 16, :].astype(jnp.int32).astype(f32)
            notes = piece[rows:]
            for k in range(rows // 16):
                place = side * half + n * rows + k * 16
                part = piece[k * 16 : (k + 1) * 16] * jnp.exp2(-notes[k : k + 1])
                whole[pl.ds(pl.multiple_of(place, 16), 16), :] = part
            if ref is mine_ref:
                loss = loss + (notes[14:15] + notes[15:16] / 16384.0)[:, :128] * jnp.exp2(-notes[13:14, :128])
    hid = out_ref.shape[0]
    in_ref[...] = whole[:hid].T
    out_ref[...] = whole[hid : 2 * hid]
    bil_ref[...] = whole[2 * hid :]
    loss_ref[...] = jnp.broadcast_to(loss * share, loss_ref.shape)


def pair_kernel(slots, foreign, first, last, groups, site_rows, depth, heavy, out_scale, *refs):
    refs = list(refs)

    def take(count):
        taken = refs[:count]
        del refs[:count]
        return taken

    meta, counts, label_ref = take(3)
    if first:
        bil_ref = take(1)[0]
        pre_refs = take(groups)
    else:
        q_ref, qt_ref, acc_in, loss_in, hit_in, found_in = take(6)
    post_refs = take(len(slots))
    z_list = list(dict.fromkeys(z for unused, z in slots))
    grad_refs = dict(zip(z_list, take(len(z_list)), strict=True))
    if first:
        q_ref, qt_ref = take(2)
    if last:
        out_ref, acc, loss_ref, hit_ref, found_ref = refs
    else:
        acc, loss_ref, hit_ref, found_ref = refs
    tile_here, member, xb = meta[0], meta[1], meta[2]
    yg = lax.rem(tile_here // depth, 4)
    zg = lax.rem(tile_here, depth)
    toward = 1 - 2 * xb
    rows = post_refs[0].shape[1]
    width = post_refs[0].shape[2]
    pre_counts = [counts[tile_here * 4 + sub_tile(xb, a) * 2] for a in (0, 1)]
    if first:
        scale = jnp.asarray(width ** (-0.5), bf16)
        for a in range(2):
            for g in range(groups):
                first_row = owner(meta, g, groups) * rows
                site = first_row + lax.broadcasted_iota(jnp.int32, (rows, width), 0)
                part = jnp.where(site < pre_counts[a], dot(pre_refs[g][a], bil_ref[...]), 0.0).astype(bf16)
                q_ref[a, pl.ds(pl.multiple_of(first_row, rows), rows), :] = part
            qt_ref[a] = (q_ref[a] * scale).T
        acc[...] = jnp.zeros_like(acc)
        loss_ref[...] = jnp.zeros_like(loss_ref)
        hit_ref[...] = jnp.zeros_like(hit_ref)
        found_ref[...] = jnp.zeros_like(found_ref)
    elif last:
        acc[...] = acc_in[...]
        loss_ref[...] = loss_in[...]
        hit_ref[...] = hit_in[...]
        found_ref[...] = found_in[...]
    j_own = lax.broadcasted_iota(jnp.int32, (rows, site_rows), 0)
    j_col = lax.broadcasted_iota(jnp.int32, (rows, 128), 0)
    i_row = lax.broadcasted_iota(jnp.int32, (1, site_rows), 1)
    step = rows // (8 if rows >= 128 else 4)
    i_ok = [i_row < count for count in pre_counts]
    if foreign:
        nz = sum(1 for dy, unused in slots if dy == 0)
        chunks = [[(n, 0) for n in range(k, k + nz)] for k in range(0, len(slots), nz)]
    else:
        chunks = [[(n, 0), (n, 1)] for n in range(len(slots))]
    for chunk in chunks:
        post = jnp.concatenate([post_refs[n][t] for n, t in chunk], 0)
        post_t = post.T
        places = []
        for n, t in chunk:
            sign, z_slot = slots[n]
            dy = sign * (1 - 2 * lax.rem(yg, 2))
            if depth == 2:
                z_other = zg if z_slot == 0 else 1 - zg
            else:
                z_other = zg + z_slot
            x_other = 1 - xb if foreign else xb
            y_other = yg + dy
            inside = (y_other >= 0) & (y_other < 4) & (z_other >= 0) & (z_other < depth)
            source = jnp.where(inside, x_other * 4 * depth + y_other * depth + z_other, tile_here)
            valid = jnp.clip(counts[source * 4 + sub_tile(x_other, t) * 2 + 1] - member * rows, 0, rows)
            places.append((t, dy, z_other - zg, jnp.where(inside, valid, 0)))
        j_bias = jnp.concatenate([jnp.where(j_col < place[3], 0.0, OFF).astype(f32) for place in places], 0)
        j_bias = jnp.concatenate([j_bias] * (site_rows // 128), 1)
        total = None
        for a in (0,) if foreign else (0, 1):
            targets = []
            for t, dy, dz, valid in places:
                dx = toward if foreign else 0 if t == a else -toward if a == 0 else toward
                base = ((dx + 1) * 9 + (dy + 1) * 3 + dz + 1) * site_rows + member * rows
                key = label_ref[sub_tile(xb, a)] - base
                key = jnp.where(i_ok[a] & (key < valid), key, -1)
                found_ref[a] += jnp.where(key >= 0, 1.0, 0.0)
                targets.append(j_own == key)
            target = jnp.concatenate(targets, 0)
            s = dot(post, qt_ref[a]) + j_bias
            e = jnp.exp(-jnp.abs(s))
            w = 1.0 + e
            r = pl.reciprocal(w, approx=True)
            chance = jnp.where(s >= 0.0, r, e * r)
            slope = jnp.where(target, (chance - 1.0) * heavy, chance).astype(bf16)
            part = dot(slope, q_ref[a])
            total = part if total is None else total + part
            acc[a] += dot(post_t, slope)
            piece = hit = None
            for k in range(len(chunk)):
                product = small = above = None
                for g in range(k * rows, (k + 1) * rows, step):
                    here = slice(g, g + step)
                    more = jnp.maximum(s[here], 0.0)
                    found = jnp.where(target[here], s[here], 0.0)
                    product = w[here] if product is None else product * w[here]
                    small = e[here] if small is None else small + e[here]
                    above = more if above is None else above + more
                    hit = found if hit is None else hit + found
                loss = above + jnp.where(small < 1e-3, small, jnp.log(product))
                piece = loss if piece is None else piece + loss
            loss_ref[...] += jnp.where(i_ok[a], jnp.sum(piece.reshape(step // 8, 8, site_rows), 0), 0.0)
            hit_ref[a] += jnp.sum(hit.reshape(step // 8, 8, site_rows), 0)
        for k, (n, t) in enumerate(chunk):
            dy, z_slot = slots[n]
            place = [other for other, z in slots if z == z_slot].index(dy) * post_refs[n].shape[0] + t
            grad_refs[z_slot][place] = total[k * rows : (k + 1) * rows] * out_scale
    if last:
        total = jnp.sum(loss_ref[...])
        for a in range(2):
            ok = lax.broadcasted_iota(jnp.int32, (site_rows, width), 0) < pre_counts[a]
            out_ref[a * site_rows : (a + 1) * site_rows] = jnp.where(ok, (acc[a] * out_scale).T, 0.0)
            score = jnp.sum(hit_ref[a], 0, keepdims=True)
            soft = jnp.log1p(jnp.exp(-jnp.abs(score)))
            missed = heavy * (jnp.maximum(-score, 0.0) + soft) - (jnp.maximum(score, 0.0) + soft)
            total = total + jnp.sum(jnp.where(found_ref[a] > 0.0, missed, 0.0))
        out_ref[2 * site_rows :] = jnp.full((8, width), total, f32)


def pair_call(name, slots, foreign, first, last, operands, posts, sizes):
    tiles, rows, width = posts[0].shape
    groups, site_rows = sizes[0], sizes[1]
    kernel = functools.partial(pair_kernel, slots, foreign, first, last, *sizes)
    state = [
        ((2, width, site_rows), f32),
        ((8, site_rows), f32),
        ((2, 8, site_rows), f32),
        ((2, 1, site_rows), f32),
    ]
    z_count = len(set(z for unused, z in slots))
    outs = [((tiles * len(slots) // z_count, rows, width), f32)] * z_count
    if first:
        outs += [((2, site_rows, width), bf16), ((2, width, site_rows), bf16)]
    if last:
        outs += [((2 * site_rows + 8, width), f32)]
    else:
        outs += state
    pairs = len(slots) * (1 if foreign else 4)
    aliases = {} if first or last else {5 + n: z_count + n for n in range(4)}
    results = call(
        kernel,
        name,
        outs,
        operands + posts,
        flops=pairs * rows * site_rows * width * 40,
        scratch=[pltpu.VMEM(shape, kind) for shape, kind in state] if last else (),
        aliases=aliases,
    )
    return list(results[:z_count]), list(results[z_count:])


def after(array, *others):
    return lax.optimization_barrier((array, *others))[0]


def local(features, w_in, w_out, bilinear, partner, counts):
    row_part = features.shape[1]
    width = features.shape[4]
    hid = w_in.shape[1]
    groups = lax.axis_size("mlp")
    site_rows = row_part * groups
    tile_count = lax.axis_size("tile")
    depth = tile_count // 8
    tile_here = lax.axis_index("tile")
    member = lax.axis_index("mlp")
    xb = tile_here // (4 * depth)
    heavy = float(27 * site_rows // 4)
    out_scale = width ** (-0.5) / (2 * tile_count * site_rows)
    half = tile_count // 2

    def side(i):
        return i ^ half

    def along_y(sign):
        def target(i):
            y = i // depth % 4
            step = sign * (1 - 2 * (y % 2))
            return i + step * depth if 0 <= y + step < 4 else None

        return target

    def both(sign):
        return lambda i: None if along_y(sign)(i) is None else along_y(sign)(i) ^ half

    z_slots = (0, 1) if depth == 2 else (0, -1, 1)

    def along_z(slot):
        if depth == 2:
            return lambda i: i ^ 1
        return lambda i: i - slot if 0 <= i % depth - slot < depth else None

    def back_z(slot):
        return along_z(slot if depth == 2 else -slot)

    def from_z(array):
        return [moved(array, "tile", along_z(slot)) for slot in z_slots[1:]]

    w_ins, w_outs = over_mlp(w_in), over_mlp(w_out)
    meta = jnp.stack([tile_here, member, xb]).astype(jnp.int32)
    x0, x1 = [jnp.transpose(features[0, :, :, kind], (1, 0, 2)) for kind in (0, 1)]
    x0s, x1s = over_mlp(x0), over_mlp(x1)
    labels = lax.dynamic_index_in_dim(partner, tile_here, 0, keepdims=False)[:, None, :]
    flat_counts = counts.reshape(-1)
    rows3 = (2, row_part, width)
    flops = 4 * row_part * width * hid * 4
    begun = call(mlp_own_kernel, "mlp_own", [(rows3, f32)] * 2, [meta, x0, x1, w_in, w_out], flops)
    pairs_w = [w for pair in zip(w_ins[1:], w_outs[1:], strict=True) for w in pair]
    more = functools.partial(mlp_kernel, True, groups - 1)
    near_shape = (1, row_part, width)
    post, post_near = call(
        more, "mlp_post", [(rows3, bf16), (near_shape, bf16)], [meta, x1, begun[1], *pairs_w], flops * (groups - 1) // 2
    )
    pre = call(more, "mlp_pre", [(rows3, bf16)], [meta, x0, begun[0], *pairs_w], flops * (groups - 1) // 2)[0]
    if groups == 2:
        full = functools.partial(mlp_kernel, False, 2)
        pres = [pre, call(full, "mlp_pre_other", [(rows3, bf16)], [meta, x0s[1], w_in, w_out, *pairs_w], flops)[0]]
    else:
        pres = over_mlp(pre)

    near = {dy: moved(post, "tile", along_y(dy)) for dy in (-1, 1)}
    far = {0: moved(post_near, "tile", side)}
    sizes = (groups, site_rows, depth, heavy, out_scale)
    fixed = [meta, flat_counts, labels]
    grads_own, (query, query_t, *state) = pair_call(
        "pairs_own", [(0, z) for z in z_slots], False, True, False, fixed + [bilinear, *pres], [post] + from_z(post), sizes
    )
    queries = [query, query_t]
    for dy in (-1, 1):
        far[dy] = moved(after(post_near, state[1]), "tile", both(dy))
    near = {dy: after(near[dy], state[1], x1s[-1]) for dy in (-1, 1)}
    near_z = {dy: from_z(near[dy]) for dy in (-1, 1)}
    grads_near, state = pair_call(
        "pairs_near", [(dy, 0) for dy in (-1, 1)], False, False, False, fixed + queries + state, [near[-1], near[1]], sizes
    )
    far = {dy: after(far[dy], state[1]) for dy in (-1, 0, 1)}
    far_z = {dy: from_z(far[dy]) for dy in (-1, 0, 1)}
    grads_near_z, state = pair_call(
        "pairs_near_z",
        [(dy, z) for dy in (-1, 1) for z in z_slots[1:]],
        False, False, False,
        fixed + queries + state,
        near_z[-1] + near_z[1],
        sizes,
    )
    grads_far, (query_part,) = pair_call(
        "pairs_far",
        [(dy, z) for dy in (-1, 0, 1) for z in z_slots],
        True, False, True,
        fixed + queries + state,
        [one for dy in (-1, 0, 1) for one in [far[dy]] + far_z[dy]],
        sizes,
    )

    def back_from_z(grads):
        return [moved(g, "tile", back_z(slot)) for slot, g in zip(z_slots[1:], grads, strict=True)]

    own_parts = grads_own[:1] + back_from_z(grads_own[1:])
    near_sums = summed(grads_near + back_from_z(grads_near_z), [(0, 2, bf16), (2, 2, bf16)], "near_sums")
    near_back = [moved(total, "tile", along_y(dy)) for total, dy in zip(near_sums, (-1, 1), strict=True)]
    query_parts = over_mlp(query_part)
    side_b, side_0, side_a = summed(
        grads_far[:1] + back_from_z(grads_far[1:]), [(0, 1, bf16), (1, 1, f32), (2, 1, bf16)], "far_sums"
    )
    side_parts = [side_0, moved(side_a, "tile", along_y(1)), moved(side_b, "tile", along_y(-1))]
    side_back = moved(summed(side_parts, [(0, 1, bf16)], "side_sum")[0], "tile", side)
    part_t = (groups, 2, hid, row_part)
    active_0, slope_0, active_1, slope_1 = call(
        functools.partial(hidden_kernel, groups),
        "hidden",
        [(part_t, bf16), (part_t, f32)] * 2,
        [meta, w_in, *x0s, *x1s],
        flops * groups // 2,
    )
    in_0, out_0, bil_0, loss = call(
        functools.partial(pre_kernel, groups),
        "pre_grads",
        [((hid, width), f32)] * 2 + [((width, width), f32), ((8, width), f32)],
        [meta, w_out, bilinear, active_0, slope_0, *query_parts, *pres, *x0s],
        flops * groups,
        [pltpu.VMEM((2, site_rows, width), bf16)] * 2,
    )
    post_back = over_mlp(summed(own_parts + near_back + [side_back], [(0, 2, bf16)], "post_sum")[0])
    half_rows = (2 * hid + width) // 2
    mine, other = call(
        functools.partial(post_kernel, groups),
        "post_grads",
        [((half_rows, width), f32), ((half_rows + 8, width), f32)],
        [meta, w_out, active_1, slope_1, in_0, out_0, bil_0, loss, *post_back, *x1s],
        flops * groups,
        [pltpu.VMEM((2 * half_rows, width), f32)],
    )

    chips = tile_count // 2
    swap = lambda i: i ^ 1
    same_core = [[core + 2 * chip for chip in range(chips)] for core in range(2)]

    def to_chips(array):
        return lax.all_to_all(array, "tile", 0, 0, tiled=True, axis_index_groups=same_core)

    half_shape, piece = (half_rows, width), (half_rows // chips + 8, width)
    sent, kept = call(
        halves_kernel,
        "halves",
        [(half_shape, bf16), (piece, f32)],
        [meta, mine, moved(other, "tile", swap), loss],
        scratch=[pltpu.VMEM(half_shape, f32)],
    )
    coded = (half_rows // chips + 16, width)
    total = call(
        total_kernel,
        "total",
        [((chips * coded[0], width), jnp.int16)],
        [meta, to_chips(sent), kept],
        scratch=[pltpu.VMEM(coded, jnp.int16)],
    )[0]
    joined = to_chips(total)
    share = 1.0 / (2.0 * tile_count * site_rows * 27 * site_rows)
    grad_in, grad_out, grad_bilinear, pair_loss = call(
        functools.partial(last_kernel, chips, share),
        "last",
        [((width, hid), f32), ((hid, width), f32), ((width, width), f32), ((8, 128), f32)],
        [meta, joined, moved(joined, "tile", swap)],
        scratch=[pltpu.VMEM((2 * half_rows, width), f32)],
    )
    return (pair_loss[0, 0], grad_in, grad_out, grad_bilinear)


def solution(mesh):
    placed = (P("tile", "mlp", None, None, None), P(None, "mlp"), P("mlp", None), P(), P(), P())
    return jax.shard_map(
        local,
        mesh=mesh,
        in_specs=placed,
        out_specs=(P(), P(None, "mlp"), P("mlp", None), P()),
        check_vma=False,
    )
```

```python
import functools

import jax
import jax.numpy as jnp
from jax import lax
from jax.experimental import pallas as pl
from jax.experimental.pallas import tpu as pltpu
from jax.sharding import PartitionSpec as P

f32 = jnp.float32
bf16 = jnp.bfloat16
OFF = -1e30
VMEM = pl.BlockSpec(memory_space=pltpu.VMEM)
SMEM = pl.BlockSpec(memory_space=pltpu.SMEM)


def dot(a, b):
    return lax.dot_general(a, b, (((1,), (0,)), ((), ())), preferred_element_type=f32)


def moved(array, axis, target):
    peers = lax.axis_size(axis)
    pairs = [(i, target(i)) for i in range(peers) if target(i) is not None]
    return lax.ppermute(array, axis, pairs)


def over_mlp(array):
    groups = lax.axis_size("mlp")
    if groups == 2:
        return [array, moved(array, "mlp", lambda i: 1 - i)]
    gathered = lax.all_gather(array, "mlp", axis=0)
    member = lax.axis_index("mlp")
    order = [lax.rem(member + step, groups) for step in range(groups)]
    return [lax.dynamic_index_in_dim(gathered, g, 0, keepdims=False) for g in order]


def owner(meta, step, groups):
    return lax.rem(meta[1] + step, groups)


def call(kernel, name, outs, operands, flops=0, scratch=(), aliases=None):
    specs = [SMEM if o.dtype == jnp.int32 and o.ndim == 1 else VMEM for o in operands]
    size = sum(o.size * o.dtype.itemsize for o in operands)
    return pl.pallas_call(
        kernel,
        out_shape=[jax.ShapeDtypeStruct(shape, kind) for shape, kind in outs],
        in_specs=specs,
        out_specs=[VMEM] * len(outs),
        scratch_shapes=list(scratch),
        input_output_aliases=aliases or {},
        compiler_params=pltpu.CompilerParams(vmem_limit_bytes=40 * 1024 * 1024),
        cost_estimate=pl.CostEstimate(flops=flops, bytes_accessed=size, transcendentals=0),
        name=name,
    )(*operands)


def summed(arrays, places, name):
    def kernel(*refs):
        for (first, count, kind), out in zip(places, refs[len(arrays) :], strict=True):
            for t in range(count):
                total = None
                for ref in refs[: len(arrays)]:
                    if first + t < ref.shape[0]:
                        part = ref[first + t].astype(f32)
                        total = part if total is None else total + part
                out[t] = total.astype(kind)

    shape = arrays[0].shape[1:]
    return call(kernel, name, [((count, *shape), kind) for unused, count, kind in places], arrays)


def sub_tile(xb, t):
    return 1 - xb if t == 0 else xb


def gelu_parts(h):
    c = 0.7978845608028654
    square = h * h
    bend = jnp.tanh(c * (h + 0.044715 * (square * h)))
    whole = 0.5 * (1.0 + bend)
    slope = whole + 0.5 * h * (1.0 - bend * bend) * (c * (1.0 + 3 * 0.044715 * square))
    return h * whole, slope


def mlp_own_kernel(meta, x0_ref, x1_ref, w_in_ref, w_out_ref, sum0_ref, sum1_ref):
    for x_ref, out_ref in ((x1_ref, sum1_ref), (x0_ref, sum0_ref)):
        for t in range(2):
            hidden = dot(x_ref[sub_tile(meta[2], t)], w_in_ref[...])
            out_ref[t] = dot(gelu_parts(hidden)[0].astype(bf16), w_out_ref[...])


def mlp_kernel(begun, groups, meta, x_ref, *refs):
    refs = list(refs)
    start_ref = refs.pop(0) if begun else None
    outs = refs[2 * groups :]
    for t in range(2):
        x = x_ref[sub_tile(meta[2], t)]
        total = start_ref[t] if begun else None
        for g in range(groups):
            hidden = dot(x, refs[2 * g][...])
            part = dot(gelu_parts(hidden)[0].astype(bf16), refs[2 * g + 1][...])
            total = part if total is None else total + part
        embedded = (x.astype(f32) + total).astype(bf16)
        outs[0][t] = embedded
        if t == 0 and len(outs) == 2:
            outs[1][0] = embedded


def hidden_kernel(groups, meta, w_in_ref, *refs):
    w_t = w_in_ref[...].T
    outs = refs[2 * groups :]
    for kind in range(2):
        for g in range(groups):
            for u in range(2):
                active, slope = gelu_parts(dot(w_t, refs[kind * groups + g][u].T))
                outs[2 * kind][g, u] = active.astype(bf16)
                outs[2 * kind + 1][g, u] = slope


def weight_part(back, x, active_t, slope_t, w_out, sums):
    active_grad = dot(w_out, back.T)
    hidden_grad = (active_grad * slope_t).astype(bf16)
    return sums[0] + dot(hidden_grad, x), sums[1] + dot(active_t, back)


def pre_kernel(groups, meta, w_out_ref, bil_ref, active_ref, slope_ref, *refs):
    query_refs, pre_refs, x_refs = refs[:groups], refs[groups : 2 * groups], refs[2 * groups : 3 * groups]
    in_ref, out_ref, bil_grad_ref, loss_ref, pre_all, back_all = refs[3 * groups :]
    rows = pre_refs[0].shape[1]
    site_rows = rows * groups
    xb = meta[2]
    bil_t = bil_ref[...].T
    bil_grad = jnp.zeros(bil_grad_ref.shape, f32)
    sums = (jnp.zeros(in_ref.shape, f32), jnp.zeros(out_ref.shape, f32))
    for a in range(2):
        total = query_refs[0][a * site_rows : (a + 1) * site_rows]
        for ref in query_refs[1:]:
            total = total + ref[a * site_rows : (a + 1) * site_rows]
        query_back = total.astype(bf16)
        for g in range(groups):
            place = pl.ds(pl.multiple_of(owner(meta, g, groups) * rows, rows), rows)
            pre_all[a, place, :] = pre_refs[g][a]
        for g in range(groups):
            place = slice(g * rows, (g + 1) * rows)
            bil_grad = bil_grad + dot(pre_all[a, place, :].T, query_back[place])
        back_all[a] = dot(query_back, bil_t).astype(bf16)
        u = sub_tile(xb, a)
        for g in range(groups):
            place = pl.ds(pl.multiple_of(owner(meta, g, groups) * rows, rows), rows)
            back = back_all[a, place, :]
            sums = weight_part(back, x_refs[g][u], active_ref[g, u], slope_ref[g, u], w_out_ref[...], sums)
    in_ref[...], out_ref[...] = sums
    bil_grad_ref[...] = bil_grad
    loss = query_refs[0][2 * site_rows :]
    for ref in query_refs[1:]:
        loss = loss + ref[2 * site_rows :]
    loss_ref[...] = loss


def post_kernel(groups, meta, w_out_ref, active_ref, slope_ref, in0, out0, bil0, loss0, *refs):
    back_refs, x_refs = refs[:groups], refs[groups : 2 * groups]
    mine_ref, other_ref, whole = refs[2 * groups :]
    xb = meta[2]
    core = lax.rem(meta[0], 2)
    sums = (in0[...], out0[...])
    for t in range(2):
        u = sub_tile(xb, t)
        for g in range(groups):
            back = back_refs[g][t]
            sums = weight_part(back, x_refs[g][u], active_ref[g, u], slope_ref[g, u], w_out_ref[...], sums)
    hid = in0.shape[0]
    half = mine_ref.shape[0]
    whole[:hid] = sums[0]
    whole[hid : 2 * hid] = sums[1]
    whole[2 * hid :] = bil0[...]
    mine_ref[...] = whole[pl.ds(pl.multiple_of(core * half, 16), half), :]
    other_ref[:half] = whole[pl.ds(pl.multiple_of((1 - core) * half, 16), half), :]
    other_ref[half:] = loss0[...]


def halves_kernel(meta, mine_ref, other_ref, loss0, sent_ref, kept_ref, whole):
    rows = kept_ref.shape[0] - 8
    half = mine_ref.shape[0]
    whole[...] = mine_ref[...] + other_ref[:half]
    sent_ref[...] = whole[...].astype(sent_ref.dtype)
    kept_ref[rows:] = loss0[...] + other_ref[half:]
    kept_ref[:rows] = whole[pl.ds(pl.multiple_of(meta[0] // 2 * rows, 16), rows), :]


def exponent(largest):
    return 14.0 - jnp.ceil(jnp.log2(jnp.maximum(largest, 1e-30)))


def total_kernel(meta, got_ref, kept_ref, out_ref, coded):
    rows = kept_ref.shape[0] - 8
    chips = got_ref.shape[0] // rows
    total = kept_ref[:rows]
    for n in range(chips):
        piece = got_ref[n * rows : (n + 1) * rows, :].astype(f32)
        total = total + jnp.where(n == meta[0] // 2, 0.0, piece)
    width = total.shape[1]
    line = lax.broadcasted_iota(jnp.int32, (16, width), 0)
    notes = jnp.zeros((16, width), f32)
    for k in range(rows // 16):
        part = total[k * 16 : (k + 1) * 16]
        power = exponent(jnp.max(jnp.max(jnp.abs(part), 0, keepdims=True), 1, keepdims=True))
        coded[k * 16 : (k + 1) * 16, :] = jnp.round(part * jnp.exp2(power)).astype(jnp.int32).astype(jnp.int16)
        notes = jnp.where(line == k, power, notes)
    loss = kept_ref[rows : rows + 1]
    power = exponent(jnp.max(loss, 1, keepdims=True))
    scaled = loss * jnp.exp2(power)
    high = jnp.floor(scaled)
    low = jnp.floor((scaled - high) * 16384.0)
    for k, note in ((13, power), (14, high), (15, low)):
        notes = jnp.where(line == k, note, notes)
    coded[rows:, :] = notes.astype(jnp.int32).astype(jnp.int16)
    for n in range(chips):
        out_ref[n * (rows + 16) : (n + 1) * (rows + 16), :] = coded[...]


def last_kernel(chips, share, meta, mine_ref, other_ref, in_ref, out_ref, bil_ref, loss_ref, whole):
    core = lax.rem(meta[0], 2)
    half = whole.shape[0] // 2
    rows = half // chips
    loss = jnp.zeros((1, 128), f32)
    for n in range(chips):
        first = n * (rows + 16)
        for ref, side in ((mine_ref, core), (other_ref, 1 - core)):
            piece = ref[first : first + rows + 16, :].astype(jnp.int32).astype(f32)
            notes = piece[rows:]
            for k in range(rows // 16):
                place = side * half + n * rows + k * 16
                part = piece[k * 16 : (k + 1) * 16] * jnp.exp2(-notes[k : k + 1])
                whole[pl.ds(pl.multiple_of(place, 16), 16), :] = part
            if ref is mine_ref:
                loss = loss + (notes[14:15] + notes[15:16] / 16384.0)[:, :128] * jnp.exp2(-notes[13:14, :128])
    hid = out_ref.shape[0]
    in_ref[...] = whole[:hid].T
    out_ref[...] = whole[hid : 2 * hid]
    bil_ref[...] = whole[2 * hid :]
    loss_ref[...] = jnp.broadcast_to(loss * share, loss_ref.shape)


def pair_kernel(slots, foreign, first, last, groups, site_rows, depth, heavy, out_scale, *refs):
    refs = list(refs)

    def take(count):
        taken = refs[:count]
        del refs[:count]
        return taken

    meta, counts, label_ref = take(3)
    if first:
        bil_ref = take(1)[0]
        pre_refs = take(groups)
    else:
        q_ref, qt_ref, acc_in, loss_in, hit_in, found_in = take(6)
    post_refs = take(len(slots))
    z_list = list(dict.fromkeys(z for unused, z in slots))
    grad_refs = dict(zip(z_list, take(len(z_list)), strict=True))
    if first:
        q_ref, qt_ref = take(2)
    if last:
        out_ref, acc, loss_ref, hit_ref, found_ref = refs
    else:
        acc, loss_ref, hit_ref, found_ref = refs
    tile_here, member, xb = meta[0], meta[1], meta[2]
    yg = lax.rem(tile_here // depth, 4)
    zg = lax.rem(tile_here, depth)
    toward = 1 - 2 * xb
    rows = post_refs[0].shape[1]
    width = post_refs[0].shape[2]
    pre_counts = [counts[tile_here * 4 + sub_tile(xb, a) * 2] for a in (0, 1)]
    if first:
        scale = jnp.asarray(width ** (-0.5), bf16)
        for a in range(2):
            for g in range(groups):
                first_row = owner(meta, g, groups) * rows
                site = first_row + lax.broadcasted_iota(jnp.int32, (rows, width), 0)
                part = jnp.where(site < pre_counts[a], dot(pre_refs[g][a], bil_ref[...]), 0.0).astype(bf16)
                q_ref[a, pl.ds(pl.multiple_of(first_row, rows), rows), :] = part
            qt_ref[a] = (q_ref[a] * scale).T
        acc[...] = jnp.zeros_like(acc)
        loss_ref[...] = jnp.zeros_like(loss_ref)
        hit_ref[...] = jnp.zeros_like(hit_ref)
        found_ref[...] = jnp.zeros_like(found_ref)
    elif last:
        acc[...] = acc_in[...]
        loss_ref[...] = loss_in[...]
        hit_ref[...] = hit_in[...]
        found_ref[...] = found_in[...]
    j_own = lax.broadcasted_iota(jnp.int32, (rows, site_rows), 0)
    j_col = lax.broadcasted_iota(jnp.int32, (rows, 128), 0)
    i_row = lax.broadcasted_iota(jnp.int32, (1, site_rows), 1)
    step = rows // (32 if rows >= 128 else 4)
    i_ok = [i_row < count for count in pre_counts]
    if foreign:
        nz = sum(1 for dy, unused in slots if dy == 0)
        chunks = [[(n, 0) for n in range(k, k + nz)] for k in range(0, len(slots), nz)]
    else:
        chunks = [[(n, 0), (n, 1)] for n in range(len(slots))]
    for chunk in chunks:
        post = jnp.concatenate([post_refs[n][t] for n, t in chunk], 0)
        post_t = post.T
        places = []
        for n, t in chunk:
            sign, z_slot = slots[n]
            dy = sign * (1 - 2 * lax.rem(yg, 2))
            if depth == 2:
                z_other = zg if z_slot == 0 else 1 - zg
            else:
                z_other = zg + z_slot
            x_other = 1 - xb if foreign else xb
            y_other = yg + dy
            inside = (y_other >= 0) & (y_other < 4) & (z_other >= 0) & (z_other < depth)
            source = jnp.where(inside, x_other * 4 * depth + y_other * depth + z_other, tile_here)
            valid = jnp.clip(counts[source * 4 + sub_tile(x_other, t) * 2 + 1] - member * rows, 0, rows)
            places.append((t, dy, z_other - zg, jnp.where(inside, valid, 0)))
        j_bias = jnp.concatenate([jnp.where(j_col < place[3], 0.0, OFF).astype(f32) for place in places], 0)
        j_bias = jnp.concatenate([j_bias] * (site_rows // 128), 1)
        total = None
        for a in (0,) if foreign else (0, 1):
            targets = []
            for t, dy, dz, valid in places:
                dx = toward if foreign else 0 if t == a else -toward if a == 0 else toward
                base = ((dx + 1) * 9 + (dy + 1) * 3 + dz + 1) * site_rows + member * rows
                key = label_ref[sub_tile(xb, a)] - base
                key = jnp.where(i_ok[a] & (key < valid), key, -1)
                found_ref[a] += jnp.where(key >= 0, 1.0, 0.0)
                targets.append(j_own == key)
            target = jnp.concatenate(targets, 0)
            s = dot(post, qt_ref[a]) + j_bias
            e = jnp.exp2(jnp.abs(s) * -1.4426950408889634)
            w = 1.0 + e
            r = pl.reciprocal(w, approx=True)
            chance = jnp.where(s >= 0.0, r, e * r)
            slope = jnp.where(target, (chance - 1.0) * heavy, chance).astype(bf16)
            part = dot(slope, q_ref[a])
            total = part if total is None else total + part
            acc[a] += dot(post_t, slope)
            piece = hit = None
            for k in range(len(chunk)):
                product = small = above = None
                for g in range(k * rows, (k + 1) * rows, step):
                    here = slice(g, g + step)
                    more = jnp.maximum(s[here], 0.0)
                    found = jnp.where(target[here], s[here], 0.0)
                    product = w[here] if product is None else product * w[here]
                    small = e[here] if small is None else small + e[here]
                    above = more if above is None else above + more
                    hit = found if hit is None else hit + found
                loss = above + jnp.where(small < 1e-3, small, jnp.log(product))
                piece = loss if piece is None else piece + loss
            loss_ref[...] += jnp.where(i_ok[a], jnp.sum(piece.reshape(step // 8, 8, site_rows), 0), 0.0)
            hit_ref[a] += jnp.sum(hit.reshape(step // 8, 8, site_rows), 0)
        for k, (n, t) in enumerate(chunk):
            dy, z_slot = slots[n]
            place = [other for other, z in slots if z == z_slot].index(dy) * post_refs[n].shape[0] + t
            grad_refs[z_slot][place] = total[k * rows : (k + 1) * rows] * out_scale
    if last:
        total = jnp.sum(loss_ref[...])
        for a in range(2):
            ok = lax.broadcasted_iota(jnp.int32, (site_rows, width), 0) < pre_counts[a]
            out_ref[a * site_rows : (a + 1) * site_rows] = jnp.where(ok, (acc[a] * out_scale).T, 0.0)
            score = jnp.sum(hit_ref[a], 0, keepdims=True)
            soft = jnp.log1p(jnp.exp(-jnp.abs(score)))
            missed = heavy * (jnp.maximum(-score, 0.0) + soft) - (jnp.maximum(score, 0.0) + soft)
            total = total + jnp.sum(jnp.where(found_ref[a] > 0.0, missed, 0.0))
        out_ref[2 * site_rows :] = jnp.full((8, width), total, f32)


def pair_call(name, slots, foreign, first, last, operands, posts, sizes):
    tiles, rows, width = posts[0].shape
    groups, site_rows = sizes[0], sizes[1]
    kernel = functools.partial(pair_kernel, slots, foreign, first, last, *sizes)
    state = [
        ((2, width, site_rows), f32),
        ((8, site_rows), f32),
        ((2, 8, site_rows), f32),
        ((2, 1, site_rows), f32),
    ]
    z_count = len(set(z for unused, z in slots))
    outs = [((tiles * len(slots) // z_count, rows, width), f32)] * z_count
    if first:
        outs += [((2, site_rows, width), bf16), ((2, width, site_rows), bf16)]
    if last:
        outs += [((2 * site_rows + 8, width), f32)]
    else:
        outs += state
    pairs = len(slots) * (1 if foreign else 4)
    aliases = {} if first or last else {5 + n: z_count + n for n in range(4)}
    results = call(
        kernel,
        name,
        outs,
        operands + posts,
        flops=pairs * rows * site_rows * width * 40,
        scratch=[pltpu.VMEM(shape, kind) for shape, kind in state] if last else (),
        aliases=aliases,
    )
    return list(results[:z_count]), list(results[z_count:])


def after(array, *others):
    return lax.optimization_barrier((array, *others))[0]


def local(features, w_in, w_out, bilinear, partner, counts):
    row_part = features.shape[1]
    width = features.shape[4]
    hid = w_in.shape[1]
    groups = lax.axis_size("mlp")
    site_rows = row_part * groups
    tile_count = lax.axis_size("tile")
    depth = tile_count // 8
    tile_here = lax.axis_index("tile")
    member = lax.axis_index("mlp")
    xb = tile_here // (4 * depth)
    heavy = float(27 * site_rows // 4)
    out_scale = width ** (-0.5) / (2 * tile_count * site_rows)
    half = tile_count // 2

    def side(i):
        return i ^ half

    def along_y(sign):
        def target(i):
            y = i // depth % 4
            step = sign * (1 - 2 * (y % 2))
            return i + step * depth if 0 <= y + step < 4 else None

        return target

    def both(sign):
        return lambda i: None if along_y(sign)(i) is None else along_y(sign)(i) ^ half

    z_slots = (0, 1) if depth == 2 else (0, -1, 1)

    def along_z(slot):
        if depth == 2:
            return lambda i: i ^ 1
        return lambda i: i - slot if 0 <= i % depth - slot < depth else None

    def back_z(slot):
        return along_z(slot if depth == 2 else -slot)

    def from_z(array):
        return [moved(array, "tile", along_z(slot)) for slot in z_slots[1:]]

    w_ins, w_outs = over_mlp(w_in), over_mlp(w_out)
    meta = jnp.stack([tile_here, member, xb]).astype(jnp.int32)
    x0, x1 = [jnp.transpose(features[0, :, :, kind], (1, 0, 2)) for kind in (0, 1)]
    x0s, x1s = over_mlp(x0), over_mlp(x1)
    labels = lax.dynamic_index_in_dim(partner, tile_here, 0, keepdims=False)[:, None, :]
    flat_counts = counts.reshape(-1)
    rows3 = (2, row_part, width)
    flops = 4 * row_part * width * hid * 4
    begun = call(mlp_own_kernel, "mlp_own", [(rows3, f32)] * 2, [meta, x0, x1, w_in, w_out], flops)
    pairs_w = [w for pair in zip(w_ins[1:], w_outs[1:], strict=True) for w in pair]
    more = functools.partial(mlp_kernel, True, groups - 1)
    near_shape = (1, row_part, width)
    post, post_near = call(
        more, "mlp_post", [(rows3, bf16), (near_shape, bf16)], [meta, x1, begun[1], *pairs_w], flops * (groups - 1) // 2
    )
    pre = call(more, "mlp_pre", [(rows3, bf16)], [meta, x0, begun[0], *pairs_w], flops * (groups - 1) // 2)[0]
    if groups == 2:
        full = functools.partial(mlp_kernel, False, 2)
        pres = [pre, call(full, "mlp_pre_other", [(rows3, bf16)], [meta, x0s[1], w_in, w_out, *pairs_w], flops)[0]]
    else:
        pres = over_mlp(pre)

    near = {dy: moved(post, "tile", along_y(dy)) for dy in (-1, 1)}
    far = {0: moved(post_near, "tile", side)}
    sizes = (groups, site_rows, depth, heavy, out_scale)
    fixed = [meta, flat_counts, labels]
    grads_own, (query, query_t, *state) = pair_call(
        "pairs_own", [(0, z) for z in z_slots], False, True, False, fixed + [bilinear, *pres], [post] + from_z(post), sizes
    )
    queries = [query, query_t]
    for dy in (-1, 1):
        far[dy] = moved(after(post_near, state[1]), "tile", both(dy))
    near = {dy: after(near[dy], state[1], x1s[-1]) for dy in (-1, 1)}
    near_z = {dy: from_z(near[dy]) for dy in (-1, 1)}
    grads_near, state = pair_call(
        "pairs_near", [(dy, 0) for dy in (-1, 1)], False, False, False, fixed + queries + state, [near[-1], near[1]], sizes
    )
    far = {dy: after(far[dy], state[1]) for dy in (-1, 0, 1)}
    far_z = {dy: from_z(far[dy]) for dy in (-1, 0, 1)}
    grads_near_z, state = pair_call(
        "pairs_near_z",
        [(dy, z) for dy in (-1, 1) for z in z_slots[1:]],
        False, False, False,
        fixed + queries + state,
        near_z[-1] + near_z[1],
        sizes,
    )
    grads_far, (query_part,) = pair_call(
        "pairs_far",
        [(dy, z) for dy in (-1, 0, 1) for z in z_slots],
        True, False, True,
        fixed + queries + state,
        [one for dy in (-1, 0, 1) for one in [far[dy]] + far_z[dy]],
        sizes,
    )

    def back_from_z(grads):
        return [moved(g, "tile", back_z(slot)) for slot, g in zip(z_slots[1:], grads, strict=True)]

    own_parts = grads_own[:1] + back_from_z(grads_own[1:])
    near_sums = summed(grads_near + back_from_z(grads_near_z), [(0, 2, bf16), (2, 2, bf16)], "near_sums")
    near_back = [moved(total, "tile", along_y(dy)) for total, dy in zip(near_sums, (-1, 1), strict=True)]
    query_parts = over_mlp(query_part)
    side_b, side_0, side_a = summed(
        grads_far[:1] + back_from_z(grads_far[1:]), [(0, 1, bf16), (1, 1, f32), (2, 1, bf16)], "far_sums"
    )
    side_parts = [side_0, moved(side_a, "tile", along_y(1)), moved(side_b, "tile", along_y(-1))]
    side_back = moved(summed(side_parts, [(0, 1, bf16)], "side_sum")[0], "tile", side)
    part_t = (groups, 2, hid, row_part)
    active_0, slope_0, active_1, slope_1 = call(
        functools.partial(hidden_kernel, groups),
        "hidden",
        [(part_t, bf16), (part_t, f32)] * 2,
        [meta, w_in, *x0s, *x1s],
        flops * groups // 2,
    )
    in_0, out_0, bil_0, loss = call(
        functools.partial(pre_kernel, groups),
        "pre_grads",
        [((hid, width), f32)] * 2 + [((width, width), f32), ((8, width), f32)],
        [meta, w_out, bilinear, active_0, slope_0, *query_parts, *pres, *x0s],
        flops * groups,
        [pltpu.VMEM((2, site_rows, width), bf16)] * 2,
    )
    post_back = over_mlp(summed(own_parts + near_back + [side_back], [(0, 2, bf16)], "post_sum")[0])
    half_rows = (2 * hid + width) // 2
    mine, other = call(
        functools.partial(post_kernel, groups),
        "post_grads",
        [((half_rows, width), f32), ((half_rows + 8, width), f32)],
        [meta, w_out, active_1, slope_1, in_0, out_0, bil_0, loss, *post_back, *x1s],
        flops * groups,
        [pltpu.VMEM((2 * half_rows, width), f32)],
    )

    chips = tile_count // 2
    swap = lambda i: i ^ 1
    same_core = [[core + 2 * chip for chip in range(chips)] for core in range(2)]

    def to_chips(array):
        return lax.all_to_all(array, "tile", 0, 0, tiled=True, axis_index_groups=same_core)

    half_shape, piece = (half_rows, width), (half_rows // chips + 8, width)
    sent, kept = call(
        halves_kernel,
        "halves",
        [(half_shape, bf16), (piece, f32)],
        [meta, mine, moved(other, "tile", swap), loss],
        scratch=[pltpu.VMEM(half_shape, f32)],
    )
    coded = (half_rows // chips + 16, width)
    total = call(
        total_kernel,
        "total",
        [((chips * coded[0], width), jnp.int16)],
        [meta, to_chips(sent), kept],
        scratch=[pltpu.VMEM(coded, jnp.int16)],
    )[0]
    joined = to_chips(total)
    share = 1.0 / (2.0 * tile_count * site_rows * 27 * site_rows)
    grad_in, grad_out, grad_bilinear, pair_loss = call(
        functools.partial(last_kernel, chips, share),
        "last",
        [((width, hid), f32), ((hid, width), f32), ((width, width), f32), ((8, 128), f32)],
        [meta, joined, moved(joined, "tile", swap)],
        scratch=[pltpu.VMEM((2 * half_rows, width), f32)],
    )
    return (pair_loss[0, 0], grad_in, grad_out, grad_bilinear)


def solution(mesh):
    placed = (P("tile", "mlp", None, None, None), P(None, "mlp"), P("mlp", None), P(), P(), P())
    return jax.shard_map(
        local,
        mesh=mesh,
        in_specs=placed,
        out_specs=(P(), P(None, "mlp"), P("mlp", None), P()),
        check_vma=False,
    )
```
